128 devices in a mesh: node: 8 (over z, core), local: 16 (over y, x).
Axes of the slice: x: 4, y: 4, z: 4, core: 2. Of those that a mesh axis runs over, the one named last changes fastest.
Arguments:
- latent_cache: bfloat16 [64, 576, 2048], P('node', None, 'local'), may hold values from -6 to 6
- lengths: int32 [64], replicated, may hold values from 512 to 2048, as said below
- owner_map: int32 [64], replicated, may hold values from 0 to 127, as said below
- queries: bfloat16 [128, 2, 73728], P(('node', 'local')), may hold values from -15 to 15, as said below
- new_latent: bfloat16 [128, 2, 576], P(('node', 'local')), may hold values from -6 to 6, as said below
- residual: bfloat16 [128, 2, 7168], P(('node', 'local')), may hold values from -6 to 6
- w_value: bfloat16 [128, 512, 128], P(('node', 'local')), may hold values from -4 to 4
- w_out: bfloat16 [16384, 7168], P(('node', 'local')), may hold values from -0.046875 to 0.046875
- norm_gain: float32 [7168], replicated, may hold values from 0.1 to 1.9
- w_router: float32 [7168, 16], replicated, may hold values from -0.0625 to 0.0625
- expert_ids: int32 [128, 2, 8], P(('node', 'local')), may hold values from 0 to 15, all different within a row
- w_gate: bfloat16 [7168, 32768], P(None, ('node', 'local')), may hold values from -0.0625 to 0.0625
- w_up: bfloat16 [7168, 32768], P(None, ('node', 'local')), may hold values from -0.0625 to 0.0625
- w_down: bfloat16 [32768, 7168], P(('node', 'local')), may hold values from -0.125 to 0.125
Outputs:
- mixed: bfloat16 [128, 2, 7168], P(('node', 'local'))
The draws below stay inside these ranges and needn't reach their ends.
Inputs may be any that keep to these rules, and one draw needn't show every extreme that they name: `lengths`: the longest request fills all 2048 positions; every request holds 512 or more. owner_map[r] is node index * 16 + local index of the device that serves request r; requests 8 * n to 8 * n + 7 are those prefilled on node n. No device serves two requests. The requests prefilled on one node are served by devices of distinct local indices, exactly 1 of them on each node, and the same 8 local indices serve on every node; local indices 0 and 15 are among them. `queries`: rows of devices that serve no request are not read. `new_latent`: rows of devices that serve no request are not read.
All inputs are finite; a program needn't handle non-finite values.
Results may differ from the reference program's by a relative error of at most 0.0095.
Values may be sent and summed in bfloat16 or wider, within the bound.
A program may use at most 128 MiB of HBM per device.

```python
import jax
import jax.numpy as jnp
from jax import lax

D = 7168
LAT = 512
H = 128
VDIM = 128
FF = 2048
NEW = 2
TOPK = 8
KDIM = 576
REQ_NODE = 8
REQUESTS = 64
LMAX = 2048
EXPERTS = 16
N_NODE = 8
N_LOCAL = 16
DEVICES = 128


def latent_noise(key):
    return jax.random.normal(jax.random.fold_in(key, 11), (DEVICES, NEW, KDIM), jnp.float32)


def draw_new_latent(key, part):
    noise_base = latent_noise(key)
    return jnp.clip(noise_base, -6.0, 6.0).astype(jnp.bfloat16)


def draw_queries(key, part):
    key = jax.random.fold_in(key, 2)
    key_drawn = jax.random.fold_in(key, 0)
    result = jnp.clip(jax.random.normal(key_drawn, (DEVICES, NEW, H, KDIM), jnp.float32), -6.0, 6.0)
    return result.reshape(DEVICES, NEW, H * KDIM).astype(jnp.bfloat16)


def draw_lengths(key, part):
    key = jax.random.fold_in(key, 3)
    key_base, key_long = jax.random.split(key)
    base_lengths = jax.random.randint(key_base, (REQUESTS,), LMAX // 4, LMAX + 1)
    longest = jax.random.randint(key_long, (), 0, REQUESTS)
    return jnp.where(jnp.arange(REQUESTS) == longest, LMAX, base_lengths).astype(jnp.int32)


def draw_owner_map(key, part):
    key = jax.random.fold_in(key, 5)
    key_nodes, key_locals, key_within = jax.random.split(key, 3)
    pair_count = REQ_NODE // N_NODE
    node_order = jax.random.permutation(key_nodes, N_NODE)
    key_middle, key_flip = jax.random.split(key_locals)
    middle_order = 1 + jax.random.permutation(key_middle, N_LOCAL - 2)
    flip_ends = jax.random.randint(key_flip, (), 0, 2)
    first_two = jnp.where(flip_ends == 0, jnp.array([N_LOCAL - 1, 0]), jnp.array([0, N_LOCAL - 1]))
    local_order = jnp.concatenate([first_two, middle_order]).astype(jnp.int32)
    node_keys = jax.random.split(key_within, N_NODE)
    within = jax.vmap(lambda node_key: jax.random.permutation(node_key, REQ_NODE))(node_keys)
    source = jnp.arange(N_NODE)[:, None]
    target = node_order[(source + within // pair_count) % N_NODE]
    return (target * N_LOCAL + local_order[within]).reshape(REQUESTS).astype(jnp.int32)


def steps_of(rng, shape, shards, low, top_value):
    def one(axis_at, parts):
        draws = jax.random.uniform(jax.random.fold_in(jax.random.fold_in(rng, 6), axis_at), (parts,), jnp.float32, low / len(shards), top_value / len(shards))
        return jnp.repeat(jnp.exp(draws), shape[axis_at] // parts).reshape((-1,) + (1,) * (len(shape) - axis_at - 1))

    loudness = one(*shards[0])
    for cut in shards[1:]:
        loudness = loudness * one(*cut)
    return loudness


def distinct(rng, rows, count, top, lift):
    order = jax.random.permutation(jax.random.fold_in(rng, 1), count)
    boost = order
    for power in range(3):
        boost = boost * boost // count
    boost = boost * lift // count
    tickets = jax.random.randint(jax.random.fold_in(rng, 2), (rows, count), 0, 4096) + boost
    sure = jax.random.permutation(jax.random.fold_in(rng, 3), rows)[jnp.arange(count) % rows]
    tickets = jnp.where(jnp.arange(rows)[:, None] == sure[None, :], 1 << 14, tickets)
    priority = tickets * count + jnp.arange(count)
    return lax.top_k(priority.astype(jnp.int32), top)[1].astype(jnp.int32)


def noise(key, shape, spread, bound, shards=(), kind=jnp.bfloat16):
    gain = steps_of(key, shape, shards, -0.22, 0.18) if shards else 1.0
    values = jax.random.normal(key, shape, jnp.float32) * spread * gain
    return jnp.minimum(jnp.maximum(values, -bound), bound).astype(kind)


def setup_inputs(seed: int = 0) -> dict:
    keys = jax.random.split(jax.random.key(seed), 15)
    latent_cache = noise(keys[0], (REQUESTS, KDIM, LMAX), 1.0, 6.0, ((0, 8), (2, 16)))
    lengths = draw_lengths(jax.random.fold_in(keys[14], 71), 0)
    owner_map = draw_owner_map(jax.random.fold_in(keys[14], 71), 0)
    queries = draw_queries(jax.random.fold_in(keys[14], 71), 0)
    new_latent = draw_new_latent(jax.random.fold_in(keys[14], 71), 0)
    residual = noise(keys[5], (DEVICES, NEW, D), 1.0, 6.0, ((0, 128),))
    w_value = noise(keys[6], (H, LAT, VDIM), 2 ** -0.5, 4.0, ((0, 128),))
    w_out = noise(keys[7], (H * VDIM, D), (H * VDIM) ** -0.5, 0.046875, ((0, 128),))
    norm_gain = jnp.clip(1.0 + 0.18 * jax.random.normal(keys[8], (D,), jnp.float32), 0.1, 1.9)
    w_router = noise(keys[9], (D, EXPERTS), D ** -0.5, 0.0625, (), jnp.float32)
    expert_ids = distinct(keys[10], DEVICES * NEW, EXPERTS, TOPK, 8192).reshape((DEVICES, NEW, TOPK))
    w_gate = noise(keys[11], (D, EXPERTS * FF), D ** -0.5, 0.0625, ((1, 128),))
    w_up = noise(keys[12], (D, EXPERTS * FF), D ** -0.5, 0.0625, ((1, 128),))
    w_down = noise(keys[13], (EXPERTS * FF, D), FF ** -0.5, 0.125, ((0, 128),))
    return dict(latent_cache=latent_cache, lengths=lengths, owner_map=owner_map, queries=queries, new_latent=new_latent, residual=residual, w_value=w_value, w_out=w_out, norm_gain=norm_gain, w_router=w_router, expert_ids=expert_ids, w_gate=w_gate, w_up=w_up, w_down=w_down)


score_scale = 192.0 ** (-0.5)
route_scale = 2.5
norm_eps = 1e-06

def attend_request(key_rows, query_rows, fresh_rows, length):
    step_count = fresh_rows.shape[0]
    key_width = fresh_rows.shape[1]
    head_count = query_rows.shape[1] // key_width
    flat_rows = query_rows.reshape(step_count * head_count, key_width)
    cached = jnp.dot(flat_rows, key_rows, preferred_element_type=jnp.float32) * score_scale
    places = jnp.arange(key_rows.shape[1], dtype=jnp.int32)
    cached = jnp.where(places[None, :] < length, cached, -jnp.inf)
    fresh_scores = lax.dot_general(flat_rows, fresh_rows, (((1,), (1,)), ((), ())), preferred_element_type=jnp.float32) * score_scale
    row_step = jnp.arange(step_count * head_count, dtype=jnp.int32) // head_count
    col_step = jnp.arange(step_count, dtype=jnp.int32)
    fresh_scores = jnp.where(col_step[None, :] <= row_step[:, None], fresh_scores, -jnp.inf)
    row_max = jnp.maximum(lax.optimization_barrier(jnp.max(cached, axis=1)), lax.optimization_barrier(jnp.max(fresh_scores, axis=1)))
    cache_weights = jnp.exp(cached - row_max[:, None])
    fresh_weights = jnp.exp(fresh_scores - row_max[:, None])
    weight_total = lax.optimization_barrier(jnp.sum(cache_weights, axis=1)) + lax.optimization_barrier(jnp.sum(fresh_weights, axis=1))
    weighted = lax.dot_general(cache_weights.astype(jnp.bfloat16), key_rows[:LAT], (((1,), (1,)), ((), ())), preferred_element_type=jnp.float32)
    weighted = weighted + jnp.dot(fresh_weights.astype(jnp.bfloat16), fresh_rows[:, :LAT], preferred_element_type=jnp.float32)
    result = (weighted / weight_total[:, None]).astype(jnp.bfloat16)
    return jnp.transpose(result.reshape(step_count, head_count, LAT), (1, 0, 2))

def reference(latent_cache, lengths, owner_map, queries, new_latent, residual, w_value, w_out, norm_gain, w_router, expert_ids, w_gate, w_up, w_down):
    request_order = jnp.arange(REQUESTS, dtype=jnp.int32)

    def per_request(request_index):
        owner_slot = owner_map[request_index]
        return attend_request(latent_cache[request_index], queries[owner_slot], new_latent[owner_slot], lengths[request_index])
    attended_rows = lax.map(per_request, request_order)
    attended = jnp.zeros((DEVICES, H, NEW, LAT), jnp.bfloat16).at[owner_map].set(attended_rows)
    head_values = jnp.einsum('dhtl,hlv->dhtv', attended.astype(jnp.float32), w_value.astype(jnp.float32)).astype(jnp.bfloat16)
    attention = jnp.einsum('dhtv,hvx->dtx', head_values.astype(jnp.float32), w_out.reshape(H, VDIM, D).astype(jnp.float32))
    hidden = (residual.astype(jnp.float32) + attention).astype(jnp.bfloat16)
    hidden_wide = hidden.astype(jnp.float32)
    normed = (hidden_wide * lax.rsqrt(lax.optimization_barrier(jnp.mean(hidden_wide * hidden_wide, axis=-1, keepdims=True)) + norm_eps) * norm_gain).astype(jnp.bfloat16)
    token_count = DEVICES * NEW
    token_rows = normed.reshape(token_count, D)
    affinity = jax.nn.sigmoid(jnp.dot(token_rows.astype(jnp.float32), w_router, precision=lax.Precision.HIGHEST))
    choose = (expert_ids.reshape(token_count, TOPK)[:, :, None] == jnp.arange(EXPERTS, dtype=jnp.int32)).astype(jnp.float32)
    picked_scores = lax.optimization_barrier(jnp.sum(affinity[:, None, :] * choose, axis=2))
    gate_weights = picked_scores / lax.optimization_barrier(jnp.sum(picked_scores, axis=1, keepdims=True)) * route_scale
    combine = lax.optimization_barrier(jnp.sum(gate_weights[:, :, None] * choose, axis=1)).astype(jnp.bfloat16)
    combine_wide = lax.optimization_barrier(combine).astype(jnp.float32)
    per_node = EXPERTS // N_NODE

    def per_node_out(node_index):

        def per_slot(total, slot):
            expert_index = node_index * per_node + slot
            first = (expert_index * FF).astype(jnp.int32)
            gate_part = lax.dynamic_slice_in_dim(w_gate, first, FF, 1)
            up_part = lax.dynamic_slice_in_dim(w_up, first, FF, 1)
            down_part = lax.dynamic_slice_in_dim(w_down, first, FF, 0)
            gated = jnp.dot(token_rows, gate_part, preferred_element_type=jnp.float32)
            lifted = jnp.dot(token_rows, up_part, preferred_element_type=jnp.float32)
            middle = (jax.nn.silu(gated) * lifted).astype(jnp.bfloat16)
            weight = lax.dynamic_slice_in_dim(combine_wide, expert_index.astype(jnp.int32), 1, 1)
            return (total + weight * jnp.dot(middle, down_part, preferred_element_type=jnp.float32), None)
        total, _ = lax.scan(per_slot, jnp.zeros((token_count, D), jnp.float32), jnp.arange(per_node, dtype=jnp.int32))
        return total.astype(jnp.bfloat16)
    node_out = lax.map(per_node_out, jnp.arange(N_NODE, dtype=jnp.int32))
    mixture = lax.optimization_barrier(jnp.sum(node_out.astype(jnp.float32), axis=0))
    mixed = (hidden_wide.reshape(token_count, D) + mixture).astype(jnp.bfloat16)
    return mixed.reshape(DEVICES, NEW, D)
```

```python
import functools

import jax
import jax.numpy as jnp
from jax import lax
from jax.experimental import pallas as pl
from jax.experimental.pallas import tpu as pltpu
from jax.sharding import PartitionSpec as P

MESH = pl.DeviceIdType.MESH
BF = jnp.bfloat16
F32 = jnp.float32
score_scale = 192.0 ** (-0.5)
route_scale = 2.5
norm_eps = 1e-06
NT = (((1,), (1,)), ((), ()))


def iota(shape, dim):
    return lax.broadcasted_iota(jnp.int32, shape, dim)


def landed(ref, sem):
    pltpu.make_async_copy(ref, ref, sem).wait()


def send(src, dst, send_sem, recv_sem, device):
    pltpu.make_async_remote_copy(
        src_ref=src, dst_ref=dst, send_sem=send_sem, recv_sem=recv_sem,
        device_id=device, device_id_type=MESH,
    ).start()


def keep(src, dst, sem):
    pltpu.make_async_copy(src, dst, sem).start()


def home_local(node, target):
    row = target // 2
    return row * 4 + (target % 2) * 2 + (row + node) % 2


def each(lo, hi, body):
    def step(i, carry):
        body(i)
        return carry
    lax.fori_loop(lo, hi, step, 0)


def attend_kernel(
    owner, lengths, cache, qc, w_value, w_out, out,
    csend, crecv, q1, q2s, q2, q3, sbuf, acc, att, c1, c2s, c2, hv, hvr, wr, ys, yr,
    cs, cr, q1s, q1r, q2ss, q2r, q3s, q3r, a1s, a1r, a2s, a2r, hs, hr, ws, wrr, yss, yrr,
):
    n = lax.axis_index("node")
    l = lax.axis_index("local")
    yy, xx, core, zz = l // 4, l % 4, n % 2, n // 2
    home_core = (xx + yy) % 2
    is_home = home_core == core

    bar = pltpu.get_barrier_semaphore()
    each(1, 16, lambda j: pl.semaphore_signal(bar, 1, device_id=(n, (l + j) % 16), device_id_type=MESH))
    each(1, 8, lambda j: pl.semaphore_signal(bar, 1, device_id=((n + j) % 8, l), device_id_type=MESH))
    pl.semaphore_wait(bar, 22)

    keep(qc.at[l], q1.at[l], q1r.at[l])

    def q_first(j):
        p = (l + j) % 16
        send(qc.at[p], q1.at[l], q1s.at[p], q1r.at[l], (n, p))
    each(1, 16, q_first)

    def cache_send(j):
        t = (l + j) % 8
        pick = jnp.int32(0)
        for i in range(8):
            pick = jnp.where(owner[n * 8 + i] // 16 == t, i, pick)
        csend[t] = cache[pick]
        dest = home_local(n, t)

        @pl.when(dest == l)
        def _():
            keep(csend.at[t], crecv.at[l], cr.at[l])

        @pl.when(dest != l)
        def _():
            send(csend.at[t], crecv.at[l], cs.at[t], cr.at[l], (n, dest))
    each(0, 8, cache_send)

    def w_send(j):
        p = (n + j) % 8
        send(w_out.at[:, pl.ds(pl.multiple_of(p * 896, 128), 896)], wr.at[n], ws.at[p], wrr.at[n], (p, l))
    keep(w_out.at[:, pl.ds(pl.multiple_of(n * 896, 128), 896)], wr.at[n], wrr.at[n])
    each(1, 8, w_send)

    each(0, 16, lambda j: landed(q1.at[j], q1r.at[j]))

    def q_second(j):
        p = (n + j) % 8
        pick = jnp.int32(0)
        for i in range(8):
            o = owner[p * 8 + i]
            pick = jnp.where(o // 16 == n, o % 16, pick)
        q2s[p] = q1[pick]

        @pl.when(p == n)
        def _():
            keep(q2s.at[p], q2.at[n], q2r.at[n])

        @pl.when(p != n)
        def _():
            send(q2s.at[p], q2.at[n], q2ss.at[p], q2r.at[n], (p, l))
    each(0, 8, q_second)

    def q_third(j):
        t = (n + j) % 8
        landed(q2.at[t], q2r.at[t])
        dest = home_local(n, t)

        @pl.when(dest == l)
        def _():
            keep(q2.at[t], q3.at[l], q3r.at[l])

        @pl.when(dest != l)
        def _():
            send(q2.at[t], q3.at[l], q3s.at[t], q3r.at[l], (n, dest))
    each(0, 8, q_third)

    @pl.when(is_home)
    def _():
        each(0, 16, lambda j: landed(q3.at[j], q3r.at[j]))
        mine = yy * 2 + xx // 2
        length = jnp.int32(0)
        for i in range(8):
            r = n * 8 + i
            length = jnp.where(owner[r] // 16 == mine, lengths[r], length)
        q = q3[...].reshape(256, 640)[:, :576]
        spread = (iota((64, 576), 1) % 64 == iota((64, 576), 0)).astype(BF)
        own_band = iota((16, 576), 1) // 64 == iota((16, 576), 0)
        fresh = []
        for t in range(2):
            wide = jnp.dot(q3[t][:, 576:640], spread, preferred_element_type=F32)
            fresh.append(jnp.sum(jnp.where(own_band, wide, 0.0), axis=0, keepdims=True))
        line = iota((128, 576), 0)
        fresh_rows = jnp.where(line == 0, fresh[0], jnp.where(line == 1, fresh[1], 0.0)).astype(BF)
        fs = lax.dot_general(q, fresh_rows, NT, preferred_element_type=F32) * score_scale
        fs = jnp.where(iota((256, 128), 1) <= iota((256, 128), 0) % 2, fs, -jnp.inf)

        def score(p, top):
            landed(crecv.at[2 * p], cr.at[2 * p])
            landed(crecv.at[2 * p + 1], cr.at[2 * p + 1])
            keys = jnp.concatenate([crecv[2 * p], crecv[2 * p + 1]], axis=1)
            s = jnp.dot(q, keys, preferred_element_type=F32) * score_scale
            s = jnp.where(p * 256 + iota((256, 256), 1) < length, s, -jnp.inf)
            sbuf[p] = s
            return jnp.maximum(top, jnp.max(s, axis=1, keepdims=True))
        top = lax.fori_loop(0, 8, score, jnp.max(fs, axis=1, keepdims=True))
        fe = jnp.exp(fs - top)
        acc[...] = jnp.dot(fe.astype(BF), fresh_rows[:, :512], preferred_element_type=F32)

        def weigh(p, total):
            e = jnp.exp(sbuf[p] - top)
            values = jnp.concatenate([crecv[2 * p, :512, :], crecv[2 * p + 1, :512, :]], axis=1)
            acc[...] += lax.dot_general(e.astype(BF), values, NT, preferred_element_type=F32)
            return total + jnp.sum(e, axis=1, keepdims=True)
        total = lax.fori_loop(0, 8, weigh, jnp.sum(fe, axis=1, keepdims=True))
        att[...] = (acc[...] / total).astype(BF).reshape(8, 32, 512)

        keep(att.at[n], c1.at[zz], a1r.at[zz])

        def head_node(j):
            p = (n + j) % 8
            send(att.at[p], c1.at[zz], a1s.at[p], a1r.at[zz], (p, l))
        each(1, 8, head_node)

    each(0, 4, lambda j: landed(c1.at[j], a1r.at[j]))
    to = iota((128, 128), 0)
    perm = (iota((128, 128), 1) == (to // 2 % 4) * 32 + (to // 8) * 2 + to % 2).astype(BF)
    c2s[...] = jnp.dot(perm, c1[...].reshape(128, 512), preferred_element_type=F32).reshape(16, 8, 512)
    keep(c2s.at[l], c2.at[l], a2r.at[l])

    def head_local(j):
        p = (l + j) % 16
        send(c2s.at[p], c2.at[l], a2s.at[p], a2r.at[l], (n, p))
    each(1, 16, head_local)
    each(0, 16, lambda j: landed(c2.at[j], a2r.at[j]))
    hv[...] = jnp.dot(
        c2[...].reshape(128, 512).astype(BF), w_value[...], preferred_element_type=F32
    ).astype(BF)
    keep(hv, hvr.at[n], hr.at[n])

    def values_out(j):
        p = (n + j) % 8
        send(hv, hvr.at[n], hs.at[p], hr.at[n], (p, l))
    each(1, 8, values_out)
    each(0, 8, lambda j: landed(wr.at[j], wrr.at[j]))
    each(0, 8, lambda j: landed(hvr.at[j], hr.at[j]))
    lhs = jnp.concatenate([hvr[j] for j in range(8)], axis=1)
    ys[...] = jnp.dot(lhs, wr[...].reshape(1024, 896), preferred_element_type=F32).reshape(16, 8, 896)
    keep(ys.at[l], yr.at[l], yrr.at[l])

    def rows_out(j):
        p = (l + j) % 16
        send(ys.at[p], yr.at[l], yss.at[p], yrr.at[l], (n, p))
    each(1, 16, rows_out)
    each(0, 16, lambda j: landed(yr.at[j], yrr.at[j]))
    tot = yr[0]
    for j in range(1, 16):
        tot = tot + yr[j]
    low = tot[:, :512]
    high = jnp.concatenate([tot[:, 512:], jnp.zeros((8, 128), F32)], axis=1)
    out[...] = jnp.concatenate([low, high], axis=0).astype(BF)

    def drain(j):
        p = (l + j) % 16
        landed(qc.at[p], q1s.at[p])
        landed(c2s.at[p], a2s.at[p])
        landed(ys.at[p], yss.at[p])
    each(1, 16, drain)

    def drain_home(t):
        @pl.when(home_local(n, t) != l)
        def _():
            landed(csend.at[t], cs.at[t])
            landed(q2.at[t], q3s.at[t])
    each(0, 8, drain_home)

    def drain_node(j):
        p = (n + j) % 8
        landed(q2s.at[p], q2ss.at[p])
        landed(hv, hs.at[p])
        landed(wr.at[p], ws.at[p])

        @pl.when(is_home)
        def _():
            landed(att.at[p], a1s.at[p])
    each(1, 8, drain_node)


def attend(owner, lengths, cache, qc, w_value, w_out):
    dma = pltpu.SemaphoreType.DMA
    vm = pl.BlockSpec(memory_space=pltpu.VMEM)
    sm = pl.BlockSpec(memory_space=pltpu.SMEM)
    return pl.pallas_call(
        attend_kernel,
        name="attend",
        out_shape=jax.ShapeDtypeStruct((16, 512), BF),
        in_specs=[sm, sm, vm, vm, vm, pl.BlockSpec(memory_space=pl.ANY)],
        out_specs=vm,
        scratch_shapes=[
            pltpu.VMEM((8, 576, 128), BF),
            pltpu.VMEM((16, 576, 128), BF),
            pltpu.VMEM((16, 16, 640), BF),
            pltpu.VMEM((8, 16, 640), BF),
            pltpu.VMEM((8, 16, 640), BF),
            pltpu.VMEM((16, 16, 640), BF),
            pltpu.VMEM((8, 256, 256), F32),
            pltpu.VMEM((256, 512), F32),
            pltpu.VMEM((8, 32, 512), BF),
            pltpu.VMEM((4, 32, 512), BF),
            pltpu.VMEM((16, 8, 512), F32),
            pltpu.VMEM((16, 8, 512), F32),
            pltpu.VMEM((128, 128), BF),
            pltpu.VMEM((8, 128, 128), BF),
            pltpu.VMEM((8, 128, 896), BF),
            pltpu.VMEM((16, 8, 896), F32),
            pltpu.VMEM((16, 8, 896), F32),
        ] + [dma((k,)) for k in (8, 16, 16, 16, 8, 8, 8, 16, 8, 4, 16, 16, 8, 8, 8, 8, 16, 16)],
        compiler_params=pltpu.CompilerParams(
            collective_id=0, has_side_effects=True, vmem_limit_bytes=40 << 20
        ),
    )(owner, lengths, cache, qc, w_value, w_out)


GATHER = (("y", "z", "x"), ("z", "x", "y"), ("x", "y", "z"), ("y", "z", "x"))
PARTS = ((0, 1280, ("x", "y", "z")), (1280, 1152, ("y", "z", "x")), (2432, 1152, ("z", "x", "y")))


def expert_kernel(
    owner, shard, resall, gain, wrt, w_gate, w_up, w_down, out,
    ag, hid, chosen, wg, wu, wd, acc, mid, ya, yb, yc, r1a, r1b, r1c, t1a, t1b, t1c,
    r2a, r2b, r2c, t2a, t2b, t2c, r3a, r3b, r3c, z16,
    ags, agr, sibs, sibr, wsem, wds, wdr, ms, mr, rs, rr, zs, zr,
):
    n = lax.axis_index("node")
    l = lax.axis_index("local")
    core = n % 2
    at = {"z": n // 2, "y": l // 4, "x": l % 4}
    sib = (at["z"] * 2 + 1 - core, l)

    def peer(axis, p):
        if axis == "z":
            return (p * 2 + core, l)
        if axis == "y":
            return (n, p * 4 + at["x"])
        return (n, at["y"] * 4 + p)

    bar = pltpu.get_barrier_semaphore()
    for a in "xyz":
        for j in range(1, 4):
            pl.semaphore_signal(bar, 1, device_id=peer(a, (at[a] + j) % 4), device_id_type=MESH)
    pl.semaphore_signal(bar, 1, device_id=sib, device_id_type=MESH)

    keep(w_gate, wg, wsem.at[0])
    keep(w_up, wu, wsem.at[1])
    own_cols = pl.ds(pl.multiple_of(core * 3584, 128), 3584)
    sib_cols = pl.ds(pl.multiple_of((1 - core) * 3584, 128), 3584)
    keep(w_down.at[:, own_cols], wd.at[0], wsem.at[2])
    for q in range(4):
        ag[core, q, at["z"], at["y"], at["x"]] = shard[:, q * 128:(q + 1) * 128]
    pl.semaphore_wait(bar, 10)

    everything = pl.ds(0, 4)

    def slab(q, s, val):
        order = GATHER[q]
        idx = []
        for a in "zyx":
            if a in order[:s]:
                idx.append(everything)
            elif a == order[s]:
                idx.append(val)
            else:
                idx.append(at[a])
        return ag.at[core, q, idx[0], idx[1], idx[2]]

    def gather_start(q, s):
        a = GATHER[q][s]
        for j in range(1, 4):
            p = (at[a] + j) % 4
            send(slab(q, s, at[a]), slab(q, s, at[a]), ags.at[q, s, p], agr.at[q, s, at[a]], peer(a, p))

    def gather_wait(q, s):
        a = GATHER[q][s]
        for j in range(1, 4):
            p = (at[a] + j) % 4
            landed(slab(q, s, p), agr.at[q, s, p])

    for q in range(4):
        gather_start(q, 0)
    send(w_down.at[:, sib_cols], wd.at[1], wds, wdr, sib)

    to = iota((128, 128), 0)
    perm = (iota((128, 128), 1) == (to % 16) * 8 + to // 16).astype(BF)

    def unpack(g):
        rows = pl.ds(pl.multiple_of(g * 16, 16), 16)
        r = jnp.dot(perm, resall[pl.ds(g * 8, 8)].reshape(128, 1024), preferred_element_type=F32).astype(BF)
        for k in range(8):
            hid[rows, k * 896:(k + 1) * 896] = r[k * 16:(k + 1) * 16, :896]
        chosen[rows, :] = r[:16, 896:]

    each(0, 4, unpack)
    for s in range(1, 3):
        for q in range(4):
            gather_wait(q, s - 1)
            gather_start(q, s)
        each(4 * s, 4 * s + 4, unpack)
    each(12, 16, unpack)
    for q in range(4):
        gather_wait(q, 2)
        send(ag.at[core, q], ag.at[core, q], sibs.at[q], sibr.at[q], sib)

    row = iota((256, 64), 0)
    req = iota((256, 64), 1)
    own = jnp.broadcast_to(owner[...], (256, 64))
    target, source = own // 16, req // 8
    line = home_local(source, target) * 16 + (source // 2) * 2 + row % 2
    place = jnp.sum(jnp.where(own == row // 2, line + 1, 0), axis=1, keepdims=True) - 1
    pick_lo = (iota((256, 256), 1) == place).astype(BF)
    pick_hi = ((iota((256, 256), 1) == place + 8) & (place >= 0)).astype(BF)

    acc[...] = jnp.zeros_like(acc)
    landed(wg, wsem.at[0])
    landed(wu, wsem.at[1])
    for q in range(4):
        landed(ag.at[1 - core, q], sibr.at[q])

    def block(k, squares):
        z, c = k // 2, k % 2
        low, high = [], []
        for q in (0, 2):
            b = jnp.concatenate(
                [ag[c, q, z].reshape(256, 128), ag[c, q + 1, z].reshape(256, 128)], axis=1
            )
            low.append(jnp.dot(pick_lo, b, preferred_element_type=F32))
            high.append(jnp.dot(pick_hi, b, preferred_element_type=F32))
        attn = jnp.concatenate([low[0], low[1], high[0], high[1][:, :128]], axis=1)
        cols = pl.ds(pl.multiple_of(k * 896, 128), 896)
        h = (hid[:, cols].astype(F32) + attn).astype(BF)
        hid[:, cols] = h
        wide = h.astype(F32)
        hg = (wide * gain[:, cols]).astype(BF)
        rows = pl.ds(pl.multiple_of(k * 896, 128), 896)
        acc[:, :256] += jnp.dot(hg, wg[rows, :], preferred_element_type=F32)
        acc[:, 256:512] += jnp.dot(hg, wu[rows, :], preferred_element_type=F32)
        acc[:, 512:] += lax.dot_general(hg, wrt[:, cols], NT, preferred_element_type=F32)
        return squares + jnp.sum(wide * wide, axis=1, keepdims=True)
    squares = lax.fori_loop(0, 8, block, jnp.zeros((256, 1), F32))
    factor = lax.rsqrt(squares * (1.0 / 7168) + norm_eps)
    gated = acc[:, :256] * factor
    lifted = acc[:, 256:512] * factor
    mid[0] = (gated * jax.nn.sigmoid(gated) * lifted).astype(BF)
    send(mid.at[0], mid.at[1], ms, mr, sib)

    three = acc[:, 512:]
    logits = three[:, :128] + three[:, 128:256] + three[:, 256:]
    affinity = jax.nn.sigmoid(logits * factor)
    picked = jnp.where(chosen[...].astype(F32) > 0.5, affinity, 0.0)
    combine = (picked / jnp.sum(picked, axis=1, keepdims=True) * route_scale).astype(BF)
    lane = iota((256, 128), 1)
    e_own, e_sib = n * 2 + l // 8, sib[0] * 2 + l // 8

    landed(wd.at[0], wsem.at[2])
    landed(wd.at[1], wdr)
    landed(mid.at[1], mr)

    i = iota((256, 256), 0)
    src = iota((256, 256), 1)
    ybuf, r1, t1 = (ya, yb, yc), (r1a, r1b, r1c), (t1a, t1b, t1c)
    r2, t2, r3 = (r2a, r2b, r2c), (t2a, t2b, t2c), (r3a, r3b, r3c)
    for k, (lo, width, order) in enumerate(PARTS):
        digit = {order[0]: i // 64, order[1]: i // 16 % 4, order[2]: i // 4 % 4}
        natural = ((digit["z"] * 2 + i // 2 % 2) * 16 + digit["y"] * 4 + digit["x"]) * 2 + i % 2
        turn = (src == natural).astype(BF)
        m0 = jnp.dot(turn, mid[0], preferred_element_type=F32).astype(BF)
        m1 = jnp.dot(turn, mid[1], preferred_element_type=F32).astype(BF)
        cw = jnp.dot(turn, combine, preferred_element_type=F32)
        w0 = jnp.sum(jnp.where(lane == e_own, cw, 0.0), axis=1, keepdims=True)
        w1 = jnp.sum(jnp.where(lane == e_sib, cw, 0.0), axis=1, keepdims=True)
        for c0 in range(0, width, 384 if width % 384 == 0 else 640):
            cn = 384 if width % 384 == 0 else 640
            a = jnp.dot(m0, wd[0, :, lo + c0:lo + c0 + cn], preferred_element_type=F32) * w0
            b = jnp.dot(m1, wd[1, :, lo + c0:lo + c0 + cn], preferred_element_type=F32) * w1
            ybuf[k][:, :, c0:c0 + cn] = (a + b).astype(BF).reshape(4, 64, cn)
        a1 = order[0]
        for j in range(1, 4):
            p = (at[a1] + j) % 4
            send(ybuf[k].at[p], r1[k].at[at[a1]], rs.at[k, 0, p], rr.at[k, 0, at[a1]], peer(a1, p))
    for k, (lo, width, order) in enumerate(PARTS):
        a1, a2 = order[0], order[1]
        tot = ybuf[k][at[a1]].astype(F32)
        for j in range(1, 4):
            p = (at[a1] + j) % 4
            landed(r1[k].at[p], rr.at[k, 0, p])
            tot = tot + r1[k][p].astype(F32)
        t1[k][...] = tot.astype(BF).reshape(4, 16, width)
        for j in range(1, 4):
            p = (at[a2] + j) % 4
            send(t1[k].at[p], r2[k].at[at[a2]], rs.at[k, 1, p], rr.at[k, 1, at[a2]], peer(a2, p))
    for k, (lo, width, order) in enumerate(PARTS):
        a2, a3 = order[1], order[2]
        tot = t1[k][at[a2]].astype(F32)
        for j in range(1, 4):
            p = (at[a2] + j) % 4
            landed(r2[k].at[p], rr.at[k, 1, p])
            tot = tot + r2[k][p].astype(F32)
        t2[k][...] = tot.astype(BF)
        for j in range(1, 4):
            p = (at[a3] + j) % 4
            send(t2[k], r3[k].at[at[a3]], rs.at[k, 2, p], rr.at[k, 2, at[a3]], peer(a3, p))
    for k, (lo, width, order) in enumerate(PARTS):
        a3 = order[2]
        tot = t2[k][...].astype(F32)
        for j in range(1, 4):
            p = (at[a3] + j) % 4
            landed(r3[k].at[p], rr.at[k, 2, p])
            tot = tot + r3[k][p].astype(F32)
        z16[core, :, lo:lo + width] = tot.astype(BF)
    send(z16.at[core], z16.at[core], zs, zr, sib)
    landed(z16.at[1 - core], zr)

    up, dn = iota((16, 16), 0), iota((16, 16), 1)
    s = n * 16 + l
    sel = ((up < 2) & (dn == (s % 8) * 2 + up)).astype(BF)
    rows = pl.ds(pl.multiple_of(s // 8 * 16, 16), 16)
    for half in range(2):
        for k, (lo, width, order) in enumerate(PARTS):
            c0 = half * 3584 + lo
            base = jnp.dot(sel, hid[rows, c0:c0 + width], preferred_element_type=F32)
            pickz = ((up < 2) & (dn == at[order[2]] * 4 + core * 2 + up)).astype(BF)
            mix = jnp.dot(pickz, z16[half, :, lo:lo + width], preferred_element_type=F32)
            out[:, c0:c0 + width] = (base + mix)[:2].astype(BF)

    for q in range(4):
        for s in range(3):
            a = GATHER[q][s]
            for j in range(1, 4):
                p = (at[a] + j) % 4
                landed(slab(q, s, at[a]), ags.at[q, s, p])
        landed(ag.at[core, q], sibs.at[q])
    landed(wd.at[1], wds)
    landed(mid.at[0], ms)
    landed(z16.at[core], zs)
    for k, (lo, width, order) in enumerate(PARTS):
        for s, buf in enumerate((ybuf[k], t1[k], t2[k])):
            for j in range(1, 4):
                p = (at[order[s]] + j) % 4
                landed(buf if s == 2 else buf.at[p], rs.at[k, s, p])


def experts(owner, shard, resall, gain, wrt, w_gate, w_up, w_down):
    dma = pltpu.SemaphoreType.DMA
    vm = pl.BlockSpec(memory_space=pltpu.VMEM)
    anywhere = pl.BlockSpec(memory_space=pl.ANY)
    widths = [w for _, w, _ in PARTS]
    return pl.pallas_call(
        expert_kernel,
        name="experts",
        out_shape=jax.ShapeDtypeStruct((2, 7168), BF),
        in_specs=[vm, vm, vm, vm, vm, anywhere, anywhere, anywhere],
        out_specs=vm,
        scratch_shapes=[
            pltpu.VMEM((2, 4, 4, 4, 4, 16, 128), BF),
            pltpu.VMEM((256, 7168), BF),
            pltpu.VMEM((256, 128), BF),
            pltpu.VMEM((7168, 256), BF),
            pltpu.VMEM((7168, 256), BF),
            pltpu.VMEM((2, 256, 3584), BF),
            pltpu.VMEM((256, 512 + 384), F32),
            pltpu.VMEM((2, 256, 256), BF),
        ]
        + [pltpu.VMEM((4, 64, w), BF) for w in widths]
        + [pltpu.VMEM((4, 64, w), BF) for w in widths]
        + [pltpu.VMEM((4, 16, w), BF) for w in widths]
        + [pltpu.VMEM((4, 16, w), BF) for w in widths]
        + [pltpu.VMEM((16, w), BF) for w in widths]
        + [pltpu.VMEM((4, 16, w), BF) for w in widths]
        + [
            pltpu.VMEM((2, 16, 3584), BF),
            dma((4, 3, 4)), dma((4, 3, 4)), dma((4,)), dma((4,)), dma((3,)),
            dma, dma, dma, dma, dma((3, 3, 4)), dma((3, 3, 4)), dma, dma,
        ],
        compiler_params=pltpu.CompilerParams(
            collective_id=1, has_side_effects=True, vmem_limit_bytes=56 << 20
        ),
    )(owner, shard, resall, gain, wrt, w_gate, w_up, w_down)


def shards(
    latent_cache, lengths, owner_map, queries, new_latent, residual, w_value, w_out,
    norm_gain, w_router, expert_ids, w_gate, w_up, w_down,
):
    q = queries.reshape(2, 128, 576).transpose(1, 0, 2).reshape(16, 16, 576)
    spare = jnp.pad(new_latent.reshape(2, 9, 64), ((0, 14), (0, 7), (0, 0)))
    qc = jnp.concatenate([q, spare], axis=2)
    chosen = (expert_ids[0][:, :, None] == jnp.arange(128, dtype=jnp.int32)).any(axis=1)
    marks = jnp.pad(chosen.astype(BF)[:, None, :], ((0, 0), (0, 7), (0, 0)))
    res = jnp.concatenate([residual.reshape(2, 8, 896), marks], axis=2).reshape(16, 1024)
    resall = lax.all_gather(res, ("node", "local"), axis=0, tiled=False)
    wt = w_router.T
    hi = lax.reduce_precision(wt, 8, 7)
    mi = lax.reduce_precision(wt - hi, 8, 7)
    lo = wt - hi - mi
    wrt = jnp.pad(jnp.stack([hi, mi, lo]), ((0, 0), (0, 112), (0, 0))).reshape(384, 7168).astype(BF)
    shard = attend(owner_map, lengths, latent_cache, qc, w_value[0], w_out)
    out = experts(
        owner_map[None, :], shard, resall, norm_gain[None, :], wrt, w_gate, w_up, w_down
    )
    return out[None]


def solution(mesh):
    both = ("node", "local")
    in_specs = (
        P("node", None, "local"), P(), P(), P(both, None, None), P(both, None, None),
        P(both, None, None), P(both, None, None), P(both, None), P(), P(),
        P(both, None, None), P(None, both), P(None, both), P(both, None),
    )
    return jax.shard_map(
        shards, mesh=mesh, in_specs=in_specs, out_specs=P(both, None, None), check_vma=False
    )
```

```python
import functools

import jax
import jax.numpy as jnp
from jax import lax
from jax.experimental import pallas as pl
from jax.experimental.pallas import tpu as pltpu
from jax.sharding import PartitionSpec as P

MESH = pl.DeviceIdType.MESH
BF = jnp.bfloat16
F32 = jnp.float32
score_scale = 192.0 ** (-0.5)
route_scale = 2.5
norm_eps = 1e-06
NT = (((1,), (1,)), ((), ()))


def iota(shape, dim):
    return lax.broadcasted_iota(jnp.int32, shape, dim)


def landed(ref, sem):
    pltpu.make_async_copy(ref, ref, sem).wait()


def send(src, dst, send_sem, recv_sem, device):
    pltpu.make_async_remote_copy(
        src_ref=src, dst_ref=dst, send_sem=send_sem, recv_sem=recv_sem,
        device_id=device, device_id_type=MESH,
    ).start()


def keep(src, dst, sem):
    pltpu.make_async_copy(src, dst, sem).start()


def home_local(node, target):
    row = target // 2
    return row * 4 + (target % 2) * 2 + (row + node) % 2


def each(lo, hi, body):
    def step(i, carry):
        body(i)
        return carry
    lax.fori_loop(lo, hi, step, 0)


GATHER = (("y", "z", "x"), ("z", "x", "y"), ("x", "y", "z"), ("y", "z", "x"))
PARTS = ((0, 1280, ("x", "y", "z")), (1280, 1152, ("y", "z", "x")), (2432, 1152, ("z", "x", "y")))
WIDTHS = tuple(w for _, w, _ in PARTS)


def row_of(owner, s, t):
    own = jnp.broadcast_to(owner, s.shape)
    served = (iota(s.shape, 1) // 8) * 16 + (own // 16) * 2 + t + 1
    found = jnp.sum(jnp.where(own == s, served, 0), axis=1, keepdims=True)
    below = jnp.sum(jnp.where(own < s, 1, 0), axis=1, keepdims=True)
    return jnp.where(found > 0, found - 1, 128 + (s[:, :1] - below) * 2 + t[:, :1])


def kernel(
    owner, lengths, ids, owner_row, qc, fresh, res, gain, router, cache, w_value, w_out, w_gate, w_up, w_down, out,
    cv, csend, crecv, qs, q1, q2s, q3, sbuf, acc, att, c1, wvr, wr, hv, hvr, ys, yr,
    rtile, rg, ag, nat, hid, marks, chosen, wg, wu, wd, wrt, facc, mid, turns,
    ya, yb, yc, r1a, r1b, r1c, t1a, t1b, t1c, r2a, r2b, r2c, t2a, t2b, t2c, r3a, r3b, r3c, z16,
    ld, cs, cr, q1ss, q1r, q2ss, q3r, a1s, a1r, vs, vr, ws, wrr, hs, hr, yss, yrr,
    rgs, rgr, rbs, rbr, ags, agr, abs_, abr, wds, wdr, ms, mr, rs, rr, zs, zr,
):
    n = lax.axis_index("node")
    l = lax.axis_index("local")
    core = n % 2
    at = {"z": n // 2, "y": l // 4, "x": l % 4}
    sib = (at["z"] * 2 + 1 - core, l)
    is_home = (at["x"] + at["y"]) % 2 == core
    mine = at["y"] * 2 + at["x"] // 2

    keep(cache, cv, ld.at[0])
    bar = pltpu.get_barrier_semaphore()

    def hello(device):
        pl.semaphore_signal(bar, 1, device_id=device, device_id_type=MESH)
    each(1, 16, lambda j: hello((n, (l + j) % 16)))
    each(1, 8, lambda j: hello(((n + j) % 8, l)))

    @pl.when(is_home & (mine != n))
    def _():
        each(0, 16, lambda j: hello((mine, j)))
    keep(w_value, wvr.at[n], vr.at[n])
    keep(w_out.at[:, pl.ds(pl.multiple_of(n * 896, 128), 896)], wr.at[n], wrr.at[n])
    keep(w_gate, wg, ld.at[1])
    keep(w_up, wu, ld.at[2])
    own_cols = pl.ds(pl.multiple_of(core * 3584, 128), 3584)
    sib_cols = pl.ds(pl.multiple_of((1 - core) * 3584, 128), 3584)
    keep(w_down.at[:, own_cols], wd.at[0], ld.at[3])

    qs[:, :, :576] = qc[...]
    qs[:, :, 576:] = jnp.zeros((16, 16, 64), BF)
    own_band = iota((16, 576), 1) // 64 == iota((16, 576), 0)
    fold = (iota((576, 64), 0) % 64 == iota((576, 64), 1)).astype(BF)
    new = fresh[...].astype(F32)
    for t in range(2):
        bands = jnp.where(own_band, jnp.broadcast_to(new[t:t + 1], (16, 576)), 0.0).astype(BF)
        qs[t, :, 576:640] = jnp.dot(bands, fold, preferred_element_type=F32).astype(BF)
    landed(cv, ld.at[0])
    pl.semaphore_wait(bar, 29)

    keep(qs.at[l], q1.at[l], q1r.at[l])

    def q_first(j):
        p = (l + j) % 16
        send(qs.at[p], q1.at[l], q1ss.at[p], q1r.at[l], (n, p))
    each(1, 16, q_first)

    def cache_send(j):
        t = (l + j) % 8
        pick = jnp.int32(0)
        for i in range(8):
            pick = jnp.where(owner[n * 8 + i] // 16 == t, i, pick)
        csend[t] = cv[pick]
        dest = home_local(n, t)

        @pl.when(dest == l)
        def _():
            keep(csend.at[t], crecv.at[l], cr.at[l])

        @pl.when(dest != l)
        def _():
            send(csend.at[t], crecv.at[l], cs.at[t], cr.at[l], (n, dest))
    each(0, 8, cache_send)

    def v_send(j):
        p = (n + j) % 8
        send(w_value, wvr.at[n], vs.at[p], vr.at[n], (p, l))
    each(1, 8, v_send)

    each(0, 16, lambda j: landed(q1.at[j], q1r.at[j]))

    def q_second(j):
        p = (n + j) % 8
        pick = jnp.int32(0)
        for i in range(8):
            o = owner[p * 8 + i]
            pick = jnp.where(o // 16 == n, o % 16, pick)
        q2s[p] = q1[pick]
        dest = home_local(p, n)
        self_ = (p == n) & (dest == l)

        @pl.when(self_)
        def _():
            keep(q2s.at[p], q3.at[l], q3r.at[l])

        @pl.when(jnp.logical_not(self_))
        def _():
            send(q2s.at[p], q3.at[l], q2ss.at[p], q3r.at[l], (p, dest))
    each(0, 8, q_second)

    def w_send(j):
        p = (n + j) % 8
        send(w_out.at[:, pl.ds(pl.multiple_of(p * 896, 128), 896)], wr.at[n], ws.at[p], wrr.at[n], (p, l))
    each(1, 8, w_send)
    send(w_down.at[:, sib_cols], wd.at[1], wds, wdr, sib)

    everything = pl.ds(0, 4)

    def peer(axis, p):
        if axis == "z":
            return (p * 2 + core, l)
        if axis == "y":
            return (n, p * 4 + at["x"])
        return (n, at["y"] * 4 + p)

    def slab(buf, q, s, val):
        order = GATHER[q]
        idx = []
        for a in "zyx":
            if a in order[:s]:
                idx.append(everything)
            elif a == order[s]:
                idx.append(val)
            else:
                idx.append(at[a])
        return buf.at[core, q, idx[0], idx[1], idx[2]]

    def gather_start(buf, ss, rs_, q, s):
        a = GATHER[q][s]
        for j in range(1, 4):
            p = (at[a] + j) % 4
            send(slab(buf, q, s, at[a]), slab(buf, q, s, at[a]), ss.at[q, s, p], rs_.at[q, s, at[a]], peer(a, p))

    def gather_wait(buf, rs_, q, s):
        a = GATHER[q][s]
        for j in range(1, 4):
            p = (at[a] + j) % 4
            landed(slab(buf, q, s, p), rs_.at[q, s, p])

    def gather_drain(buf, ss):
        for q in range(4):
            for s in range(3):
                a = GATHER[q][s]
                for j in range(1, 4):
                    p = (at[a] + j) % 4
                    landed(slab(buf, q, s, at[a]), ss.at[q, s, p])

    r = res[...].astype(F32)
    line = iota((16, 896), 0)
    tile = jnp.zeros((16, 896), F32)
    mark = jnp.zeros((16, 128), F32)
    for t in range(2):
        for k in range(8):
            tile = jnp.where(line == t * 8 + k, jnp.broadcast_to(r[t:t + 1, k * 896:(k + 1) * 896], (16, 896)), tile)
        hit = iota((16, 128), 1) == ids[t, 0]
        for j in range(1, 8):
            hit = hit | (iota((16, 128), 1) == ids[t, j])
        mark = jnp.where(hit & (iota((16, 128), 0) == t * 8), 1.0, mark)
    rtile[...] = jnp.concatenate([tile, mark], axis=1).astype(BF)
    for q in range(4):
        rg[core, q, at["z"], at["y"], at["x"]] = rtile[:, q * 256:(q + 1) * 256]
        gather_start(rg, rgs, rgr, q, 0)

    wt = router[...]
    hi = wt.astype(BF)
    rest = wt - hi.astype(F32)
    mi = rest.astype(BF)
    wrt[0:16, :] = hi
    wrt[16:32, :] = mi
    wrt[32:48, :] = (rest - mi.astype(F32)).astype(BF)
    wrt[48:128, :] = jnp.zeros((80, 7168), BF)

    i64 = iota((256, 64), 0)
    spot = row_of(owner_row[...], i64 // 2, i64 % 2)
    to_nat = jnp.where(iota((256, 256), 1) == spot, 1.0, 0.0)
    turns[3] = to_nat.T.astype(BF)
    for k, (lo, width, order) in enumerate(PARTS):
        digit = {order[0]: i64 // 64, order[1]: i64 // 16 % 4, order[2]: i64 // 4 % 4}
        s64 = (digit["z"] * 2 + i64 // 2 % 2) * 16 + digit["y"] * 4 + digit["x"]
        turns[k] = (iota((256, 256), 1) == row_of(owner_row[...], s64, i64 % 2)).astype(BF)

    for q in range(4):
        gather_wait(rg, rgr, q, 0)
        gather_start(rg, rgs, rgr, q, 1)

    @pl.when(is_home)
    def _():
        each(0, 16, lambda j: landed(q3.at[j], q3r.at[j]))
        length = jnp.int32(0)
        for i in range(8):
            r = n * 8 + i
            length = jnp.where(owner[r] // 16 == mine, lengths[r], length)
        q = q3[...].reshape(256, 640)[:, :576]
        spread = (iota((64, 576), 1) % 64 == iota((64, 576), 0)).astype(BF)
        rows = []
        for t in range(2):
            wide = jnp.dot(q3[t][:, 576:640], spread, preferred_element_type=F32)
            rows.append(jnp.sum(jnp.where(own_band, wide, 0.0), axis=0, keepdims=True))
        up = iota((128, 576), 0)
        fresh_rows = jnp.where(up == 0, rows[0], jnp.where(up == 1, rows[1], 0.0)).astype(BF)
        fs = lax.dot_general(q, fresh_rows, NT, preferred_element_type=F32) * score_scale
        fs = jnp.where(iota((256, 128), 1) <= iota((256, 128), 0) % 2, fs, -jnp.inf)

        def score(p, top):
            landed(crecv.at[2 * p], cr.at[2 * p])
            landed(crecv.at[2 * p + 1], cr.at[2 * p + 1])
            keys = jnp.concatenate([crecv[2 * p], crecv[2 * p + 1]], axis=1)
            s = jnp.dot(q, keys, preferred_element_type=F32) * score_scale
            s = jnp.where(p * 256 + iota((256, 256), 1) < length, s, -jnp.inf)
            sbuf[p] = s
            return jnp.maximum(top, jnp.max(s, axis=1, keepdims=True))
        top = lax.fori_loop(0, 8, score, jnp.max(fs, axis=1, keepdims=True))
        fe = jnp.exp(fs - top)
        acc[...] = jnp.dot(fe.astype(BF), fresh_rows[:, :512], preferred_element_type=F32)

        def weigh(p, total):
            e = jnp.exp(sbuf[p] - top)
            values = jnp.concatenate([crecv[2 * p, :512, :], crecv[2 * p + 1, :512, :]], axis=1)
            acc[...] += lax.dot_general(e.astype(BF), values, NT, preferred_element_type=F32)
            return total + jnp.sum(e, axis=1, keepdims=True)
        total = lax.fori_loop(0, 8, weigh, jnp.sum(fe, axis=1, keepdims=True))
        att[...] = (acc[...] / total).astype(BF).reshape(16, 16, 512)

        keep(att.at[l], c1.at[mine], a1r.at[mine])

        def head_local(j):
            p = (l + j) % 16
            send(att.at[p], c1.at[mine], a1s.at[p], a1r.at[mine], (n, p))
        each(1, 16, head_local)

    for q in range(4):
        gather_wait(rg, rgr, q, 1)
        gather_start(rg, rgs, rgr, q, 2)

    each(0, 8, lambda j: landed(wvr.at[j], vr.at[j]))
    each(0, 8, lambda j: landed(c1.at[j], a1r.at[j]))
    to = iota((128, 128), 0)
    perm = (iota((128, 128), 1) == (to // 2 % 8) * 16 + (to // 16) * 2 + to % 2).astype(BF)
    by_head = jnp.dot(perm, c1[...].reshape(128, 512), preferred_element_type=F32).astype(BF)
    for k in range(8):
        hv[:, k * 128:(k + 1) * 128] = jnp.dot(
            by_head[k * 16:(k + 1) * 16], wvr[k], preferred_element_type=F32
        ).astype(BF)
    keep(hv, hvr.at[n], hr.at[n])

    def values_out(j):
        p = (n + j) % 8
        send(hv, hvr.at[n], hs.at[p], hr.at[n], (p, l))
    each(1, 8, values_out)
    each(0, 8, lambda j: landed(wr.at[j], wrr.at[j]))
    each(0, 8, lambda j: landed(hvr.at[j], hr.at[j]))
    proj = jnp.dot(
        hvr[...].reshape(128, 1024), wr[...].reshape(1024, 896), preferred_element_type=F32
    ).reshape(16, 8, 896)
    high = jnp.concatenate([proj[:, :, 512:], jnp.zeros((16, 8, 128), F32)], axis=2)
    ys[...] = jnp.concatenate([proj[:, :, :512], high], axis=1).astype(BF)
    keep(ys.at[l], yr.at[l], yrr.at[l])

    def rows_out(j):
        p = (l + j) % 16
        send(ys.at[p], yr.at[l], yss.at[p], yrr.at[l], (n, p))
    each(1, 16, rows_out)
    for q in range(4):
        gather_wait(rg, rgr, q, 2)
        send(rg.at[core, q], rg.at[core, q], rbs.at[q], rbr.at[q], sib)
    each(0, 16, lambda j: landed(yr.at[j], yrr.at[j]))
    tot = yr[0].astype(F32)
    for j in range(1, 16):
        tot = tot + yr[j].astype(F32)
    shard = tot.astype(BF)
    for q in range(4):
        ag[core, q, at["z"], at["y"], at["x"]] = shard[:, q * 128:(q + 1) * 128]
        gather_start(ag, ags, agr, q, 0)

    for q in range(4):
        landed(rg.at[1 - core, q], rbr.at[q])
    deal = (iota((128, 128), 1) == (to % 16) * 8 + to // 16).astype(BF)

    def unpack(g):
        rows = pl.ds(pl.multiple_of(g * 16, 16), 16)
        z, c, y2 = g // 4, g // 2 % 2, g % 2
        x = jnp.concatenate(
            [rg[c, q, z, pl.ds(y2 * 2, 2)].reshape(128, 256) for q in range(4)], axis=1
        )
        d = jnp.dot(deal, x, preferred_element_type=F32).astype(BF)
        for k in range(8):
            nat[rows, k * 896:(k + 1) * 896] = d[k * 16:(k + 1) * 16, :896]
        marks[rows, :] = d[:16, 896:]

    def reorder(k):
        cols = pl.ds(pl.multiple_of(k * 896, 128), 896)
        hid[:, cols] = jnp.dot(turns[3], nat[:, cols], preferred_element_type=F32).astype(BF)

    each(0, 8, unpack)
    for q in range(4):
        gather_wait(ag, agr, q, 0)
        gather_start(ag, ags, agr, q, 1)
    each(8, 16, unpack)
    for q in range(4):
        gather_wait(ag, agr, q, 1)
        gather_start(ag, ags, agr, q, 2)
    each(0, 8, reorder)
    chosen[...] = jnp.dot(turns[3], marks[...], preferred_element_type=F32)
    facc[...] = jnp.zeros_like(facc)
    landed(wg, ld.at[1])
    landed(wu, ld.at[2])
    for q in range(4):
        gather_wait(ag, agr, q, 2)
        send(ag.at[core, q], ag.at[core, q], abs_.at[q], abr.at[q], sib)
    for q in range(4):
        landed(ag.at[1 - core, q], abr.at[q])

    def block(k, squares):
        z, c = k // 2, k % 2
        tops, lows = [], []
        for q in range(4):
            b = ag[c, q, z].reshape(16, 16, 128).astype(F32)
            tops.append(b[:, :8].reshape(128, 128))
            lows.append(b[:, 8:].reshape(128, 128))
        attn = jnp.concatenate(tops + lows[:3], axis=1)
        cols = pl.ds(pl.multiple_of(k * 896, 128), 896)
        wide = hid[:, cols].astype(F32)
        h = jnp.concatenate([wide[:128] + attn, wide[128:]], axis=0).astype(BF)
        hid[:, cols] = h
        wide = h.astype(F32)
        hg = (wide * gain[:, cols]).astype(BF)
        rows = pl.ds(pl.multiple_of(k * 896, 128), 896)
        facc[:, :256] += jnp.dot(hg, wg[rows, :], preferred_element_type=F32)
        facc[:, 256:512] += jnp.dot(hg, wu[rows, :], preferred_element_type=F32)
        facc[:, 512:] += lax.dot_general(hg, wrt[:, cols], NT, preferred_element_type=F32)
        return squares + jnp.sum(wide * wide, axis=1, keepdims=True)
    squares = lax.fori_loop(0, 8, block, jnp.zeros((256, 1), F32))
    factor = lax.rsqrt(squares * (1.0 / 7168) + norm_eps)
    gated = facc[:, :256] * factor
    lifted = facc[:, 256:512] * factor
    mid[0] = (gated * jax.nn.sigmoid(gated) * lifted).astype(BF)
    send(mid.at[0], mid.at[1], ms, mr, sib)

    three = facc[:, 512:]
    logits = three + pltpu.roll(three, 112, 1) + pltpu.roll(three, 96, 1)
    affinity = jax.nn.sigmoid(logits * factor)
    picked = jnp.where(chosen[...] > 0.5, affinity, 0.0)
    combine = (picked / jnp.sum(picked, axis=1, keepdims=True) * route_scale).astype(BF)
    lane = iota((256, 128), 1)
    e_own, e_sib = n * 2 + l // 8, sib[0] * 2 + l // 8
    landed(wd.at[0], ld.at[3])
    landed(wd.at[1], wdr)
    landed(mid.at[1], mr)

    ybuf, r1, t1 = (ya, yb, yc), (r1a, r1b, r1c), (t1a, t1b, t1c)
    r2, t2, r3 = (r2a, r2b, r2c), (t2a, t2b, t2c), (r3a, r3b, r3c)
    for k, (lo, width, order) in enumerate(PARTS):
        m0 = jnp.dot(turns[k], mid[0], preferred_element_type=F32).astype(BF)
        m1 = jnp.dot(turns[k], mid[1], preferred_element_type=F32).astype(BF)
        cw = jnp.dot(turns[k], combine, preferred_element_type=F32)
        w0 = jnp.sum(jnp.where(lane == e_own, cw, 0.0), axis=1, keepdims=True)
        w1 = jnp.sum(jnp.where(lane == e_sib, cw, 0.0), axis=1, keepdims=True)
        cn = 384 if width % 384 == 0 else 640
        for c0 in range(0, width, cn):
            a = jnp.dot(m0, wd[0, :, lo + c0:lo + c0 + cn], preferred_element_type=F32) * w0
            b = jnp.dot(m1, wd[1, :, lo + c0:lo + c0 + cn], preferred_element_type=F32) * w1
            ybuf[k][:, :, c0:c0 + cn] = (a + b).astype(BF).reshape(4, 64, cn)
        a1 = order[0]
        for j in range(1, 4):
            p = (at[a1] + j) % 4
            send(ybuf[k].at[p], r1[k].at[at[a1]], rs.at[k, 0, p], rr.at[k, 0, at[a1]], peer(a1, p))

    s16 = iota((16, 64), 0) * 0 + (n * 16 + l)
    own_rows = row_of(owner_row[...], s16, iota((16, 64), 0) % 2)
    sel = (iota((16, 256), 1) == own_rows).astype(BF)

    for k, (lo, width, order) in enumerate(PARTS):
        a1, a2 = order[0], order[1]
        tot = ybuf[k][at[a1]].astype(F32)
        for j in range(1, 4):
            p = (at[a1] + j) % 4
            landed(r1[k].at[p], rr.at[k, 0, p])
            tot = tot + r1[k][p].astype(F32)
        t1[k][...] = tot.astype(BF).reshape(4, 16, width)
        for j in range(1, 4):
            p = (at[a2] + j) % 4
            send(t1[k].at[p], r2[k].at[at[a2]], rs.at[k, 1, p], rr.at[k, 1, at[a2]], peer(a2, p))
    for k, (lo, width, order) in enumerate(PARTS):
        a2, a3 = order[1], order[2]
        tot = t1[k][at[a2]].astype(F32)
        for j in range(1, 4):
            p = (at[a2] + j) % 4
            landed(r2[k].at[p], rr.at[k, 1, p])
            tot = tot + r2[k][p].astype(F32)
        t2[k][...] = tot.astype(BF)
        for j in range(1, 4):
            p = (at[a3] + j) % 4
            send(t2[k], r3[k].at[at[a3]], rs.at[k, 2, p], rr.at[k, 2, at[a3]], peer(a3, p))
    for k, (lo, width, order) in enumerate(PARTS):
        a3 = order[2]
        tot = t2[k][...].astype(F32)
        for j in range(1, 4):
            p = (at[a3] + j) % 4
            landed(r3[k].at[p], rr.at[k, 2, p])
            tot = tot + r3[k][p].astype(F32)
        z16[core, :, lo:lo + width] = tot.astype(BF)
    send(z16.at[core], z16.at[core], zs, zr, sib)
    landed(z16.at[1 - core], zr)

    up, dn = iota((16, 16), 0), iota((16, 16), 1)
    for half in range(2):
        for k, (lo, width, order) in enumerate(PARTS):
            c0 = half * 3584 + lo
            base = jnp.dot(sel, hid[:, c0:c0 + width], preferred_element_type=F32)
            pickz = ((up < 2) & (dn == at[order[2]] * 4 + core * 2 + up)).astype(BF)
            mix = jnp.dot(pickz, z16[half, :, lo:lo + width], preferred_element_type=F32)
            out[:, c0:c0 + width] = (base + mix)[:2].astype(BF)

    def drain(j):
        p = (l + j) % 16
        landed(qs.at[p], q1ss.at[p])
        landed(ys.at[p], yss.at[p])

        @pl.when(is_home)
        def _():
            landed(att.at[p], a1s.at[p])
    each(1, 16, drain)

    def drain_home(t):
        @pl.when(home_local(n, t) != l)
        def _():
            landed(csend.at[t], cs.at[t])

        @pl.when(jnp.logical_not((t == n) & (home_local(t, n) == l)))
        def _():
            landed(q2s.at[t], q2ss.at[t])
    each(0, 8, drain_home)

    def drain_node(j):
        p = (n + j) % 8
        landed(wvr.at[p], vs.at[p])
        landed(hv, hs.at[p])
        landed(wr.at[p], ws.at[p])
    each(1, 8, drain_node)
    gather_drain(rg, rgs)
    gather_drain(ag, ags)
    for q in range(4):
        landed(rg.at[core, q], rbs.at[q])
        landed(ag.at[core, q], abs_.at[q])
    landed(wd.at[1], wds)
    landed(mid.at[0], ms)
    landed(z16.at[core], zs)
    for k, (lo, width, order) in enumerate(PARTS):
        for s, buf in enumerate((ybuf[k], t1[k], t2[k])):
            for j in range(1, 4):
                p = (at[order[s]] + j) % 4
                landed(buf if s == 2 else buf.at[p], rs.at[k, s, p])


def layer(owner, lengths, ids, qc, fresh, res, gain, router, cache, w_value, w_out, w_gate, w_up, w_down):
    dma = pltpu.SemaphoreType.DMA
    vm = pl.BlockSpec(memory_space=pltpu.VMEM)
    sm = pl.BlockSpec(memory_space=pltpu.SMEM)
    hbm = pl.BlockSpec(memory_space=pl.ANY)
    bf = lambda *shape: pltpu.VMEM(shape, BF)
    f32 = lambda *shape: pltpu.VMEM(shape, F32)
    return pl.pallas_call(
        kernel,
        name="layer",
        out_shape=jax.ShapeDtypeStruct((2, 7168), BF),
        in_specs=[sm, sm, sm, vm, vm, vm, vm, vm, vm, hbm, hbm, hbm, hbm, hbm, hbm],
        out_specs=vm,
        scratch_shapes=[
            bf(8, 576, 128), bf(8, 576, 128), bf(16, 576, 128),
            bf(16, 16, 640), bf(16, 16, 640), bf(8, 16, 640), bf(16, 16, 640),
            f32(8, 256, 256), f32(256, 512), bf(16, 16, 512), bf(8, 16, 512),
            bf(8, 512, 128), bf(8, 128, 896), bf(16, 1024), bf(8, 16, 1024),
            bf(16, 16, 512), bf(16, 16, 512),
            bf(16, 1024), bf(2, 4, 4, 4, 4, 16, 256), bf(2, 4, 4, 4, 4, 16, 128),
            bf(256, 7168), bf(256, 7168), bf(256, 128), f32(256, 128),
            bf(7168, 256), bf(7168, 256), bf(2, 256, 3584), bf(128, 7168),
            f32(256, 640), bf(2, 256, 256), bf(4, 256, 256),
        ]
        + [bf(4, 64, w) for w in WIDTHS] + [bf(4, 64, w) for w in WIDTHS]
        + [bf(4, 16, w) for w in WIDTHS] + [bf(4, 16, w) for w in WIDTHS]
        + [bf(16, w) for w in WIDTHS] + [bf(4, 16, w) for w in WIDTHS]
        + [bf(2, 16, 3584)]
        + [dma((k,)) for k in (4, 8, 16, 16, 16, 8, 16, 16, 8, 8, 8, 8, 8, 8, 8, 16, 16)]
        + [
            dma((4, 3, 4)), dma((4, 3, 4)), dma((4,)), dma((4,)),
            dma((4, 3, 4)), dma((4, 3, 4)), dma((4,)), dma((4,)),
            dma, dma, dma, dma, dma((3, 3, 4)), dma((3, 3, 4)), dma, dma,
        ],
        compiler_params=pltpu.CompilerParams(
            collective_id=0, has_side_effects=True, vmem_limit_bytes=58 << 20
        ),
    )(owner, lengths, ids, owner[None, :], qc, fresh, res, gain, router, cache, w_value, w_out, w_gate, w_up, w_down)


def shards(
    latent_cache, lengths, owner_map, queries, new_latent, residual, w_value, w_out,
    norm_gain, w_router, expert_ids, w_gate, w_up, w_down,
):
    qc = queries.reshape(2, 8, 16, 576).transpose(2, 1, 0, 3).reshape(16, 16, 576)
    out = layer(
        owner_map, lengths, expert_ids[0], qc, new_latent[0], residual[0], norm_gain[None, :], w_router.T,
        latent_cache, w_value[0], w_out, w_gate, w_up, w_down,
    )
    return out[None]


def solution(mesh):
    both = ("node", "local")
    in_specs = (
        P("node", None, "local"), P(), P(), P(both, None, None), P(both, None, None),
        P(both, None, None), P(both, None, None), P(both, None), P(), P(),
        P(both, None, None), P(None, both), P(None, both), P(both, None),
    )
    return jax.shard_map(
        shards, mesh=mesh, in_specs=in_specs, out_specs=P(both, None, None), check_vma=False
    )
```

```python
import functools

import jax
import jax.numpy as jnp
from jax import lax
from jax.experimental import pallas as pl
from jax.experimental.pallas import tpu as pltpu
from jax.sharding import PartitionSpec as P

MESH = pl.DeviceIdType.MESH
BF = jnp.bfloat16
F32 = jnp.float32
score_scale = 192.0 ** (-0.5)
route_scale = 2.5
norm_eps = 1e-06
NT = (((1,), (1,)), ((), ()))


def iota(shape, dim):
    return lax.broadcasted_iota(jnp.int32, shape, dim)


def landed(ref, sem):
    pltpu.make_async_copy(ref, ref, sem).wait()


def send(src, dst, send_sem, recv_sem, device):
    pltpu.make_async_remote_copy(
        src_ref=src, dst_ref=dst, send_sem=send_sem, recv_sem=recv_sem,
        device_id=device, device_id_type=MESH,
    ).start()


def keep(src, dst, sem):
    pltpu.make_async_copy(src, dst, sem).start()


def home_local(node, target):
    row = target // 2
    return row * 4 + (target % 2) * 2 + (row + node) % 2


def each(lo, hi, body):
    def step(i, carry):
        body(i)
        return carry
    lax.fori_loop(lo, hi, step, 0)


GATHER = (("y", "z", "x"), ("z", "x", "y"), ("x", "y", "z"), (("y", "z", "x"), ("z", "x", "y")))
RESIDUAL = (("z", "y", "x"), ("z", "x", "y"), ("z", "y", "x"), ("z", "x", "y"))
CACHE_FIRST = 4
RG0_EARLY = 1
V_EARLY = 1
RG1_AT = 1
RG2_AT = (1, 1, 1, 1)
EVEN = ((1, 1), (3, 3), (1, 3), (3, 1), (2, 0), (0, 2), (2, 2), (0, 0))
ODD = ((1, 0), (3, 0), (0, 1), (0, 3), (1, 2), (3, 2), (2, 1), (2, 3))
UNPACK_FIRST = 12
PARTS = ((0, 1280, ("x", "y", "z")), (1280, 1152, ("y", "z", "x")), (2432, 1152, ("z", "x", "y")))
WIDTHS = tuple(w for _, w, _ in PARTS)


def row_of(owner, s, t):
    own = jnp.broadcast_to(owner, s.shape)
    served = (iota(s.shape, 1) // 8) * 16 + (own // 16) * 2 + t + 1
    found = jnp.sum(jnp.where(own == s, served, 0), axis=1, keepdims=True)
    below = jnp.sum(jnp.where(own < s, 1, 0), axis=1, keepdims=True)
    return jnp.where(found > 0, found - 1, 128 + (s[:, :1] - below) * 2 + t[:, :1])


def kernel(
    owner, lengths, ids, owner_hbm, queries_hbm, fresh_hbm, res_hbm, gain_hbm, router_hbm, cache, w_value, w_out, w_gate, w_up, w_down, out,
    owner_row, queries, fresh, res, gain, router, cv, csend, crecv, qf, qs, q1, q2s, q3, sbuf, acc, att, c1, wvr, wr, hv, hvr, ys, yr,
    rtile, rg, ag, nat, hid, marks, chosen, wg, wu, wd, wrt, facc, mid, combine, base, turns,
    ya, yb, yc, r1a, r1b, r1c, t1a, t1b, t1c, r2a, r2b, r2c, t2a, t2b, t2c, r3a, r3b, r3c, z16,
    ld, cs, cr, q1ss, q1r, q2ss, q3r, a1s, a1r, vs, vr, vbs, vbr, ws, wrr, hs, hr, yss, yrr,
    rgs, rgr, rbs, rbr, ags, agr, abs_, abr, wds, wdr, ms, mr, rs, rr, zs, zr,
):
    n = lax.axis_index("node")
    l = lax.axis_index("local")
    core = n % 2
    at = {"z": n // 2, "y": l // 4, "x": l % 4}
    sib = (at["z"] * 2 + 1 - core, l)
    is_home = (at["x"] + at["y"]) % 2 == core
    mine = at["y"] * 2 + at["x"] // 2

    everything = pl.ds(0, 4)

    def peer(axis, p):
        if axis == "z":
            return (p * 2 + core, l)
        if axis == "y":
            return (n, p * 4 + at["x"])
        return (n, at["y"] * 4 + p)

    def slab(buf, order, q, s, val):
        idx = []
        for a in "zyx":
            if a in order[:s]:
                idx.append(everything)
            elif a == order[s]:
                idx.append(val)
            else:
                idx.append(at[a])
        return buf.at[core, q, idx[0], idx[1], idx[2]]

    def by_core(order, body):
        if isinstance(order[0], str):
            body(order)
        else:
            for c in range(2):
                pl.when(core == c)(functools.partial(body, order[c]))

    def gather_start(buf, orders, ss, rs_, q, s):
        def body(order):
            a = order[s]
            own = slab(buf, order, q, s, at[a])
            for j in range(1, 4):
                p = (at[a] + j) % 4
                send(own, own, ss.at[q, s, p], rs_.at[q, s, at[a]], peer(a, p))
        by_core(orders[q], body)

    def gather_wait(buf, orders, rs_, q, s):
        def body(order):
            a = order[s]
            for j in range(1, 4):
                p = (at[a] + j) % 4
                landed(slab(buf, order, q, s, p), rs_.at[q, s, p])
        by_core(orders[q], body)

    def gather_drain(buf, orders, ss):
        for q in range(4):
            def body(order, q=q):
                for s in range(3):
                    a = order[s]
                    for j in range(1, 4):
                        p = (at[a] + j) % 4
                        landed(slab(buf, order, q, s, at[a]), ss.at[q, s, p])
            by_core(orders[q], body)

    bar = pltpu.get_barrier_semaphore()

    def hello(device):
        pl.semaphore_signal(bar, 1, device_id=device, device_id_type=MESH)
    each(1, 16, lambda j: hello((n, (l + j) % 16)))
    each(1, 8, lambda j: hello(((n + j) % 8, l)))

    @pl.when(is_home & (mine != n))
    def _():
        each(0, 16, lambda j: hello((mine, j)))
    small = ((queries_hbm, queries), (fresh_hbm, fresh), (res_hbm, res), (owner_hbm, owner_row))
    for j, (src, dst) in enumerate(small):
        keep(src, dst, ld.at[4 + j])
    keep(cache, cv, ld.at[0])
    keep(router_hbm, router, ld.at[8])
    keep(gain_hbm, gain, ld.at[9])
    keep(w_value, wvr.at[at["z"], core], vr.at[at["z"]])
    keep(w_out.at[:, pl.ds(pl.multiple_of(n * 896, 128), 896)], wr.at[n], wrr.at[n])
    keep(w_gate, wg, ld.at[1])
    keep(w_up, wu, ld.at[2])
    own_cols = pl.ds(pl.multiple_of(core * 3584, 128), 3584)
    sib_cols = pl.ds(pl.multiple_of((1 - core) * 3584, 128), 3584)
    keep(w_down.at[:, own_cols], wd.at[0], ld.at[3])

    def deal_queries(pair):
        for k in range(8):
            lanes = pl.ds(pl.multiple_of((k * 8 + pair) * 1152, 128), 1152)
            v = queries[:, lanes].astype(F32)
            qf[pair * 2, k * 2:k * 2 + 2, :576] = v[:, :576]
            qf[pair * 2 + 1, k * 2:k * 2 + 2, :576] = v[:, 576:]
    for j, (src, dst) in enumerate(small):
        landed(dst, ld.at[4 + j])
    each(0, 8, deal_queries)
    qs[:, :, :576] = qf[:, :, :576].astype(BF)
    qs[:, :, 576:] = jnp.zeros((16, 16, 64), BF)
    own_band = iota((16, 576), 1) // 64 == iota((16, 576), 0)
    fold = (iota((576, 64), 0) % 64 == iota((576, 64), 1)).astype(BF)
    new = fresh[...].astype(F32)
    for t in range(2):
        bands = jnp.where(own_band, jnp.broadcast_to(new[t:t + 1], (16, 576)), 0.0).astype(BF)
        qs[t, :, 576:640] = jnp.dot(bands, fold, preferred_element_type=F32).astype(BF)

    r = res[...].astype(F32)
    line = iota((16, 896), 0)
    tile = jnp.zeros((16, 896), F32)
    mark = jnp.zeros((16, 128), F32)
    for t in range(2):
        for k in range(8):
            tile = jnp.where(line == t * 8 + k, jnp.broadcast_to(r[t:t + 1, k * 896:(k + 1) * 896], (16, 896)), tile)
        hit = iota((16, 128), 1) == ids[t, 0]
        for j in range(1, 8):
            hit = hit | (iota((16, 128), 1) == ids[t, j])
        mark = jnp.where(hit & (iota((16, 128), 0) == t * 8), 1.0, mark)
    rtile[...] = jnp.concatenate([tile, mark], axis=1).astype(BF)
    for q in range(4):
        rg[core, q, at["z"], at["y"], at["x"]] = rtile[:, q * 256:(q + 1) * 256]

    landed(cv, ld.at[0])

    def cache_pick(t):
        pick = jnp.int32(0)
        for i in range(8):
            pick = jnp.where(owner[n * 8 + i] // 16 == t, i, pick)
        csend[t] = cv[pick]
    each(0, 8, cache_pick)
    pl.semaphore_wait(bar, 29)

    keep(qs.at[l], q1.at[l], q1r.at[l])

    def q_first(j):
        p = (l + j) % 16
        send(qs.at[p], q1.at[l], q1ss.at[p], q1r.at[l], (n, p))
    each(1, 16, q_first)
    if RG0_EARLY:
        for q in range(4):
            gather_start(rg, RESIDUAL, rgs, rgr, q, 0)

    def cache_send(i):
        dx = jnp.where(is_home, EVEN[i][0], ODD[i][0])
        dy = jnp.where(is_home, EVEN[i][1], ODD[i][1])
        px, py = (at["x"] + dx) % 4, (at["y"] + dy) % 4
        t, dest = py * 2 + px // 2, py * 4 + px

        @pl.when(dest == l)
        def _():
            keep(csend.at[t], crecv.at[l], cr.at[l])

        @pl.when(dest != l)
        def _():
            send(csend.at[t], crecv.at[l], cs.at[t], cr.at[l], (n, dest))
    for i in range(CACHE_FIRST):
        cache_send(i)

    def v_send():
        for j in range(1, 4):
            p = (at["z"] + j) % 4
            send(w_value, wvr.at[at["z"], core], vs.at[p], vr.at[at["z"]], peer("z", p))
    if V_EARLY:
        v_send()

    each(0, 16, lambda j: landed(q1.at[j], q1r.at[j]))

    def q_second(j):
        p = (n + j) % 8
        pick = jnp.int32(0)
        for i in range(8):
            o = owner[p * 8 + i]
            pick = jnp.where(o // 16 == n, o % 16, pick)
        q2s[p] = q1[pick]
        dest = home_local(p, n)
        self_ = (p == n) & (dest == l)

        @pl.when(self_)
        def _():
            keep(q2s.at[p], q3.at[l], q3r.at[l])

        @pl.when(jnp.logical_not(self_))
        def _():
            send(q2s.at[p], q3.at[l], q2ss.at[p], q3r.at[l], (p, dest))
    each(0, 8, q_second)
    for i in range(CACHE_FIRST, 8):
        cache_send(i)

    if not V_EARLY:
        v_send()
    if not RG0_EARLY:
        for q in range(4):
            gather_start(rg, RESIDUAL, rgs, rgr, q, 0)

    def w_send(j):
        p = (n + j) % 8
        send(w_out.at[:, pl.ds(pl.multiple_of(p * 896, 128), 896)], wr.at[n], ws.at[p], wrr.at[n], (p, l))
    each(1, 8, w_send)
    send(w_down.at[:, sib_cols], wd.at[1], wds, wdr, sib)
    def rg1():
        for q in range(4):
            gather_wait(rg, RESIDUAL, rgr, q, 0)
            gather_start(rg, RESIDUAL, rgs, rgr, q, 1)

    def rg2(phase):
        for q in range(4):
            if RG2_AT[q] == phase:
                gather_wait(rg, RESIDUAL, rgr, q, 1)
                gather_start(rg, RESIDUAL, rgs, rgr, q, 2)
    if RG1_AT == 0:
        rg1()

    landed(router, ld.at[8])
    landed(gain, ld.at[9])
    wt = router[...]
    hi = wt.astype(BF)
    rest = wt - hi.astype(F32)
    mi = rest.astype(BF)
    wrt[0:16, :] = hi
    wrt[16:32, :] = mi
    wrt[32:48, :] = (rest - mi.astype(F32)).astype(BF)
    wrt[48:128, :] = jnp.zeros((80, 7168), BF)

    i64 = iota((256, 64), 0)
    spot = row_of(owner_row[...], i64 // 2, i64 % 2)
    to_nat = jnp.where(iota((256, 256), 1) == spot, 1.0, 0.0)
    turns[3] = to_nat.T.astype(BF)
    for k, (lo, width, order) in enumerate(PARTS):
        digit = {order[0]: i64 // 64, order[1]: i64 // 16 % 4, order[2]: i64 // 4 % 4}
        s64 = (digit["z"] * 2 + i64 // 2 % 2) * 16 + digit["y"] * 4 + digit["x"]
        turns[k] = (iota((256, 256), 1) == row_of(owner_row[...], s64, i64 % 2)).astype(BF)

    for j in range(4):
        landed(wvr.at[j, core], vr.at[j])
    send(wvr.at[:, core], wvr.at[:, core], vbs, vbr, sib)

    def cache_left(t):
        @pl.when(home_local(n, t) != l)
        def _():
            landed(csend.at[t], cs.at[t])
    each(0, 8, cache_left)

    @pl.when(is_home)
    def _():
        each(0, 16, lambda j: landed(crecv.at[j], cr.at[j]))
    if RG1_AT == 1:
        rg1()
    rg2(0)

    @pl.when(is_home)
    def _():
        each(0, 16, lambda j: landed(q3.at[j], q3r.at[j]))
        length = jnp.int32(0)
        for i in range(8):
            r = n * 8 + i
            length = jnp.where(owner[r] // 16 == mine, lengths[r], length)
        q = q3[...].reshape(256, 640)[:, :576]
        spread = (iota((64, 576), 1) % 64 == iota((64, 576), 0)).astype(BF)
        rows = []
        for t in range(2):
            wide = jnp.dot(q3[t][:, 576:640], spread, preferred_element_type=F32)
            rows.append(jnp.sum(jnp.where(own_band, wide, 0.0), axis=0, keepdims=True))
        up = iota((128, 576), 0)
        fresh_rows = jnp.where(up == 0, rows[0], jnp.where(up == 1, rows[1], 0.0)).astype(BF)
        fs = lax.dot_general(q, fresh_rows, NT, preferred_element_type=F32) * score_scale
        fs = jnp.where(iota((256, 128), 1) <= iota((256, 128), 0) % 2, fs, -jnp.inf)

        def score(p, top):
            keys = jnp.concatenate([crecv[2 * p], crecv[2 * p + 1]], axis=1)
            s = jnp.dot(q, keys, preferred_element_type=F32) * score_scale
            s = jnp.where(p * 256 + iota((256, 256), 1) < length, s, -jnp.inf)
            sbuf[p] = s
            return jnp.maximum(top, jnp.max(s, axis=1, keepdims=True))
        top = lax.fori_loop(0, 8, score, jnp.max(fs, axis=1, keepdims=True))
        fe = jnp.exp(fs - top)
        acc[...] = jnp.dot(fe.astype(BF), fresh_rows[:, :512], preferred_element_type=F32)

        def weigh(p, total):
            e = jnp.exp(sbuf[p] - top)
            values = jnp.concatenate([crecv[2 * p, :512, :], crecv[2 * p + 1, :512, :]], axis=1)
            acc[...] += lax.dot_general(e.astype(BF), values, NT, preferred_element_type=F32)
            return total + jnp.sum(e, axis=1, keepdims=True)
        total = lax.fori_loop(0, 8, weigh, jnp.sum(fe, axis=1, keepdims=True))
        att[...] = (acc[...] / total).astype(BF).reshape(16, 16, 512)

        keep(att.at[l], c1.at[mine], a1r.at[mine])

        def head_local(j):
            p = (l + j) % 16
            send(att.at[p], c1.at[mine], a1s.at[p], a1r.at[mine], (n, p))
        each(1, 16, head_local)

    if RG1_AT == 2:
        rg1()
    rg2(1)

    landed(wvr.at[:, 1 - core], vbr)
    each(0, 8, lambda j: landed(c1.at[j], a1r.at[j]))
    to = iota((128, 128), 0)
    perm = (iota((128, 128), 1) == (to // 2 % 8) * 16 + (to // 16) * 2 + to % 2).astype(BF)
    by_head = jnp.dot(perm, c1[...].reshape(128, 512), preferred_element_type=F32).astype(BF)
    for k in range(8):
        hv[:, k * 128:(k + 1) * 128] = jnp.dot(
            by_head[k * 16:(k + 1) * 16], wvr[k // 2, k % 2], preferred_element_type=F32
        ).astype(BF)
    keep(hv, hvr.at[n], hr.at[n])

    def values_out(j):
        p = (n + j) % 8
        send(hv, hvr.at[n], hs.at[p], hr.at[n], (p, l))
    each(1, 8, values_out)
    rg2(2)

    def rg_sib(last):
        for q in range(4):
            if (RG2_AT[q] <= 1) != last:
                gather_wait(rg, RESIDUAL, rgr, q, 2)
                send(rg.at[core, q], rg.at[core, q], rbs.at[q], rbr.at[q], sib)
    rg_sib(False)
    each(0, 8, lambda j: landed(wr.at[j], wrr.at[j]))
    each(0, 8, lambda j: landed(hvr.at[j], hr.at[j]))
    proj = jnp.dot(
        hvr[...].reshape(128, 1024), wr[...].reshape(1024, 896), preferred_element_type=F32
    ).reshape(16, 8, 896)
    high = jnp.concatenate([proj[:, :, 512:], jnp.zeros((16, 8, 128), F32)], axis=2)
    ys[...] = jnp.concatenate([proj[:, :, :512], high], axis=1).astype(BF)
    keep(ys.at[l], yr.at[l], yrr.at[l])

    def rows_out(j):
        p = (l + j) % 16
        send(ys.at[p], yr.at[l], yss.at[p], yrr.at[l], (n, p))
    each(1, 16, rows_out)
    rg2(3)

    deal = (iota((128, 128), 1) == (to % 16) * 8 + to // 16).astype(BF)

    def unpack(g):
        rows = pl.ds(pl.multiple_of(g * 16, 16), 16)
        z, c, y2 = g // 4, g // 2 % 2, g % 2
        x = jnp.concatenate(
            [rg[c, q, z, pl.ds(y2 * 2, 2)].reshape(128, 256) for q in range(4)], axis=1
        )
        d = jnp.dot(deal, x, preferred_element_type=F32).astype(BF)
        for k in range(8):
            nat[rows, k * 896:(k + 1) * 896] = d[k * 16:(k + 1) * 16, :896]
        marks[rows, :] = d[:16, 896:]

    def reorder(k):
        cols = pl.ds(pl.multiple_of(k * 896, 128), 896)
        hid[:, cols] = jnp.dot(turns[3], nat[:, cols], preferred_element_type=F32).astype(BF)

    def products(half, k, wide):
        cols = pl.ds(pl.multiple_of(k * 896, 128), 896)
        hg = (wide * gain[:, cols]).astype(BF)
        rows = pl.ds(half * 128, 128)
        facc[rows, :256] += jnp.dot(hg, wg[cols, :], preferred_element_type=F32)
        facc[rows, 256:512] += jnp.dot(hg, wu[cols, :], preferred_element_type=F32)
        facc[rows, 512:] += lax.dot_general(hg, wrt[:, cols], NT, preferred_element_type=F32)
        return jnp.sum(wide * wide, axis=1, keepdims=True)

    def activate(half, squares):
        rows = pl.ds(half * 128, 128)
        factor = lax.rsqrt(squares * (1.0 / 7168) + norm_eps)
        gated = facc[rows, :256] * factor
        lifted = facc[rows, 256:512] * factor
        mid[0, half] = (gated * jax.nn.sigmoid(gated) * lifted).astype(BF)
        send(mid.at[0, half], mid.at[1, half], ms.at[half], mr.at[half], sib)
        three = facc[rows, 512:]
        logits = three + pltpu.roll(three, 112, 1) + pltpu.roll(three, 96, 1)
        affinity = jax.nn.sigmoid(logits * factor)
        picked = jnp.where(chosen[rows, :] > 0.5, affinity, 0.0)
        share = picked / jnp.sum(picked, axis=1, keepdims=True) * route_scale
        combine[rows, :] = share.astype(BF)

    def resting(k, squares):
        cols = pl.ds(pl.multiple_of(k * 896, 128), 896)
        return squares + products(1, k, hid[128:, cols].astype(F32))

    facc[...] = jnp.zeros_like(facc)
    if UNPACK_FIRST:
        rg_sib(True)
        for q in range(4):
            landed(rg.at[1 - core, q], rbr.at[q])
    each(0, UNPACK_FIRST, unpack)
    each(0, 16, lambda j: landed(yr.at[j], yrr.at[j]))
    tot = yr[0].astype(F32)
    for j in range(1, 16):
        tot = tot + yr[j].astype(F32)
    shard = tot.astype(BF)
    for q in range(4):
        ag[core, q, at["z"], at["y"], at["x"]] = shard[:, q * 128:(q + 1) * 128]
        gather_start(ag, GATHER, ags, agr, q, 0)
    if not UNPACK_FIRST:
        rg_sib(True)
        for q in range(4):
            landed(rg.at[1 - core, q], rbr.at[q])
    each(UNPACK_FIRST, 16, unpack)
    for q in range(4):
        gather_wait(ag, GATHER, agr, q, 0)
        gather_start(ag, GATHER, ags, agr, q, 1)
    each(0, 8, reorder)
    for q in range(4):
        gather_wait(ag, GATHER, agr, q, 1)
        gather_start(ag, GATHER, ags, agr, q, 2)
    chosen[...] = jnp.dot(turns[3], marks[...], preferred_element_type=F32)
    landed(wg, ld.at[1])
    landed(wu, ld.at[2])
    activate(1, lax.fori_loop(0, 8, resting, jnp.zeros((128, 1), F32)))
    for q in range(4):
        gather_wait(ag, GATHER, agr, q, 2)
        send(ag.at[core, q], ag.at[core, q], abs_.at[q], abr.at[q], sib)

    def serving(c):
        def step(z, squares):
            tops, lows = [], []
            for q in range(4):
                b = ag[c, q, z].reshape(16, 16, 128).astype(F32)
                tops.append(b[:, :8].reshape(128, 128))
                lows.append(b[:, 8:].reshape(128, 128))
            attn = jnp.concatenate(tops + lows[:3], axis=1)
            k = z * 2 + c
            cols = pl.ds(pl.multiple_of(k * 896, 128), 896)
            h = (hid[:128, cols].astype(F32) + attn).astype(BF)
            hid[:128, cols] = h
            return squares + products(0, k, h.astype(F32))
        return step
    squares = lax.fori_loop(0, 4, serving(core), jnp.zeros((128, 1), F32))
    for q in range(4):
        landed(ag.at[1 - core, q], abr.at[q])
    activate(0, lax.fori_loop(0, 4, serving(1 - core), squares))

    lane = iota((256, 128), 1)
    e_own, e_sib = n * 2 + l // 8, sib[0] * 2 + l // 8
    landed(wd.at[0], ld.at[3])
    landed(wd.at[1], wdr)
    for half in range(2):
        landed(mid.at[1, half], mr.at[half])

    ybuf, r1, t1 = (ya, yb, yc), (r1a, r1b, r1c), (t1a, t1b, t1c)
    r2, t2, r3 = (r2a, r2b, r2c), (t2a, t2b, t2c), (r3a, r3b, r3c)
    for k, (lo, width, order) in enumerate(PARTS):
        m0 = jnp.dot(turns[k], mid[0].reshape(256, 256), preferred_element_type=F32).astype(BF)
        m1 = jnp.dot(turns[k], mid[1].reshape(256, 256), preferred_element_type=F32).astype(BF)
        cw = jnp.dot(turns[k], combine[...], preferred_element_type=F32)
        w0 = jnp.sum(jnp.where(lane == e_own, cw, 0.0), axis=1, keepdims=True)
        w1 = jnp.sum(jnp.where(lane == e_sib, cw, 0.0), axis=1, keepdims=True)
        cn = 384 if width % 384 == 0 else 640
        for c0 in range(0, width, cn):
            a = jnp.dot(m0, wd[0, :, lo + c0:lo + c0 + cn], preferred_element_type=F32) * w0
            b = jnp.dot(m1, wd[1, :, lo + c0:lo + c0 + cn], preferred_element_type=F32) * w1
            ybuf[k][:, :, c0:c0 + cn] = (a + b).astype(BF).reshape(4, 64, cn)
        a1 = order[0]
        for j in range(1, 4):
            p = (at[a1] + j) % 4
            send(ybuf[k].at[p], r1[k].at[at[a1]], rs.at[k, 0, p], rr.at[k, 0, at[a1]], peer(a1, p))

    s16 = iota((16, 64), 0) * 0 + (n * 16 + l)
    own_rows = row_of(owner_row[...], s16, iota((16, 64), 0) % 2)
    sel = (iota((16, 256), 1) == own_rows).astype(BF)
    for k in range(4):
        base[:, k * 1792:(k + 1) * 1792] = jnp.dot(
            sel, hid[:, k * 1792:(k + 1) * 1792], preferred_element_type=F32
        )

    for k, (lo, width, order) in enumerate(PARTS):
        a1, a2 = order[0], order[1]
        tot = ybuf[k][at[a1]].astype(F32)
        for j in range(1, 4):
            p = (at[a1] + j) % 4
            landed(r1[k].at[p], rr.at[k, 0, p])
            tot = tot + r1[k][p].astype(F32)
        t1[k][...] = tot.astype(BF).reshape(4, 16, width)
        for j in range(1, 4):
            p = (at[a2] + j) % 4
            send(t1[k].at[p], r2[k].at[at[a2]], rs.at[k, 1, p], rr.at[k, 1, at[a2]], peer(a2, p))
    for k, (lo, width, order) in enumerate(PARTS):
        a2, a3 = order[1], order[2]
        tot = t1[k][at[a2]].astype(F32)
        for j in range(1, 4):
            p = (at[a2] + j) % 4
            landed(r2[k].at[p], rr.at[k, 1, p])
            tot = tot + r2[k][p].astype(F32)
        t2[k][...] = tot.astype(BF)
        for j in range(1, 4):
            p = (at[a3] + j) % 4
            send(t2[k], r3[k].at[at[a3]], rs.at[k, 2, p], rr.at[k, 2, at[a3]], peer(a3, p))
    for k, (lo, width, order) in enumerate(PARTS):
        a3 = order[2]
        tot = t2[k][...].astype(F32)
        for j in range(1, 4):
            p = (at[a3] + j) % 4
            landed(r3[k].at[p], rr.at[k, 2, p])
            tot = tot + r3[k][p].astype(F32)
        z16[core, :, lo:lo + width] = tot.astype(BF)
    send(z16.at[core], z16.at[core], zs, zr, sib)
    landed(z16.at[1 - core], zr)

    up, dn = iota((16, 16), 0), iota((16, 16), 1)
    for half in range(2):
        for k, (lo, width, order) in enumerate(PARTS):
            c0 = half * 3584 + lo
            pickz = ((up < 2) & (dn == at[order[2]] * 4 + core * 2 + up)).astype(BF)
            mix = jnp.dot(pickz, z16[half, :, lo:lo + width], preferred_element_type=F32)
            out[:, c0:c0 + width] = (base[:, c0:c0 + width] + mix)[:2].astype(BF)

    def drain(j):
        p = (l + j) % 16
        landed(qs.at[p], q1ss.at[p])
        landed(ys.at[p], yss.at[p])

        @pl.when(is_home)
        def _():
            landed(att.at[p], a1s.at[p])
    each(1, 16, drain)

    def drain_home(t):
        @pl.when(jnp.logical_not((t == n) & (home_local(t, n) == l)))
        def _():
            landed(q2s.at[t], q2ss.at[t])
    each(0, 8, drain_home)

    def drain_node(j):
        p = (n + j) % 8
        landed(hv, hs.at[p])
        landed(wr.at[p], ws.at[p])
    each(1, 8, drain_node)
    for j in range(1, 4):
        p = (at["z"] + j) % 4
        landed(wvr.at[p, core], vs.at[p])
    landed(wvr.at[:, core], vbs)
    gather_drain(rg, RESIDUAL, rgs)
    gather_drain(ag, GATHER, ags)
    for q in range(4):
        landed(rg.at[core, q], rbs.at[q])
        landed(ag.at[core, q], abs_.at[q])
    landed(wd.at[1], wds)
    for half in range(2):
        landed(mid.at[0, half], ms.at[half])
    landed(z16.at[core], zs)
    for k, (lo, width, order) in enumerate(PARTS):
        for s, buf in enumerate((ybuf[k], t1[k], t2[k])):
            for j in range(1, 4):
                p = (at[order[s]] + j) % 4
                landed(buf if s == 2 else buf.at[p], rs.at[k, s, p])


def layer(owner, lengths, ids, queries, fresh, res, gain, router, cache, w_value, w_out, w_gate, w_up, w_down):
    dma = pltpu.SemaphoreType.DMA
    vm = pl.BlockSpec(memory_space=pltpu.VMEM)
    sm = pl.BlockSpec(memory_space=pltpu.SMEM)
    hbm = pl.BlockSpec(memory_space=pl.ANY)
    bf = lambda *shape: pltpu.VMEM(shape, BF)
    f32 = lambda *shape: pltpu.VMEM(shape, F32)
    return pl.pallas_call(
        kernel,
        name="layer",
        out_shape=jax.ShapeDtypeStruct((2, 7168), BF),
        in_specs=[sm, sm, sm] + [hbm] * 12,
        out_specs=vm,
        scratch_shapes=[
            pltpu.VMEM((1, 64), jnp.int32), bf(2, 73728), bf(2, 576), bf(2, 7168), f32(1, 7168), f32(16, 7168),
            bf(8, 576, 128), bf(8, 576, 128), bf(16, 576, 128),
            f32(16, 16, 640), bf(16, 16, 640), bf(16, 16, 640), bf(8, 16, 640), bf(16, 16, 640),
            f32(8, 256, 256), f32(256, 512), bf(16, 16, 512), bf(8, 16, 512),
            bf(4, 2, 512, 128), bf(8, 128, 896), bf(16, 1024), bf(8, 16, 1024),
            bf(16, 16, 512), bf(16, 16, 512),
            bf(16, 1024), bf(2, 4, 4, 4, 4, 16, 256), bf(2, 4, 4, 4, 4, 16, 128),
            bf(256, 7168), bf(256, 7168), bf(256, 128), f32(256, 128),
            bf(7168, 256), bf(7168, 256), bf(2, 256, 3584), bf(128, 7168),
            f32(256, 640), bf(2, 2, 128, 256), bf(256, 128), f32(16, 7168), bf(4, 256, 256),
        ]
        + [bf(4, 64, w) for w in WIDTHS] + [bf(4, 64, w) for w in WIDTHS]
        + [bf(4, 16, w) for w in WIDTHS] + [bf(4, 16, w) for w in WIDTHS]
        + [bf(16, w) for w in WIDTHS] + [bf(4, 16, w) for w in WIDTHS]
        + [bf(2, 16, 3584)]
        + [dma((k,)) for k in (10, 8, 16, 16, 16, 8, 16, 16, 8, 4, 4)]
        + [dma, dma]
        + [dma((k,)) for k in (8, 8, 8, 8, 16, 16)]
        + [
            dma((4, 3, 4)), dma((4, 3, 4)), dma((4,)), dma((4,)),
            dma((4, 3, 4)), dma((4, 3, 4)), dma((4,)), dma((4,)),
            dma, dma, dma((2,)), dma((2,)), dma((3, 3, 4)), dma((3, 3, 4)), dma, dma,
        ],
        compiler_params=pltpu.CompilerParams(
            collective_id=0, has_side_effects=True, vmem_limit_bytes=58 << 20
        ),
    )(owner, lengths, ids, owner[None, :], queries, fresh, res, gain, router, cache, w_value, w_out, w_gate, w_up, w_down)


def shards(
    latent_cache, lengths, owner_map, queries, new_latent, residual, w_value, w_out,
    norm_gain, w_router, expert_ids, w_gate, w_up, w_down,
):
    out = layer(
        owner_map, lengths, expert_ids[0], queries[0], new_latent[0], residual[0], norm_gain[None, :], w_router.T,
        latent_cache, w_value[0], w_out, w_gate, w_up, w_down,
    )
    return out[None]


def solution(mesh):
    both = ("node", "local")
    in_specs = (
        P("node", None, "local"), P(), P(), P(both, None, None), P(both, None, None),
        P(both, None, None), P(both, None, None), P(both, None), P(), P(),
        P(both, None, None), P(None, both), P(None, both), P(both, None),
    )
    return jax.shard_map(
        shards, mesh=mesh, in_specs=in_specs, out_specs=P(both, None, None), check_vma=False
    )
```

```python
import functools

import jax
import jax.numpy as jnp
from jax import lax
from jax.experimental import pallas as pl
from jax.experimental.pallas import tpu as pltpu
from jax.sharding import PartitionSpec as P

MESH = pl.DeviceIdType.MESH
BF = jnp.bfloat16
F32 = jnp.float32
score_scale = 192.0 ** (-0.5)
route_scale = 2.5
norm_eps = 1e-06
NT = (((1,), (1,)), ((), ()))


def iota(shape, dim):
    return lax.broadcasted_iota(jnp.int32, shape, dim)


def landed(ref, sem):
    pltpu.make_async_copy(ref, ref, sem).wait()


def send(src, dst, send_sem, recv_sem, device):
    pltpu.make_async_remote_copy(
        src_ref=src, dst_ref=dst, send_sem=send_sem, recv_sem=recv_sem,
        device_id=device, device_id_type=MESH,
    ).start()


def keep(src, dst, sem):
    pltpu.make_async_copy(src, dst, sem).start()


def home_local(node, target):
    row = target // 2
    return row * 4 + (target % 2) * 2 + (row + node) % 2


def each(lo, hi, body):
    def step(i, carry):
        body(i)
        return carry
    lax.fori_loop(lo, hi, step, 0)


GATHER = (("y", "z", "x"), ("z", "x", "y"), ("x", "y", "z"), (("y", "z", "x"), ("z", "x", "y")))
RESIDUAL = (("z", "y", "x"), ("z", "x", "y"), ("z", "y", "x"), ("z", "x", "y"))
CACHE_FIRST = 5
RG0_EARLY = 1
V_EARLY = 1
RG1_AT = 1
RG2_AT = (1, 1, 1, 1)
EVEN = ((1, 1), (3, 3), (1, 3), (3, 1), (2, 0), (0, 2), (2, 2), (0, 0))
ODD = ((1, 0), (3, 0), (0, 1), (0, 3), (1, 2), (3, 2), (2, 1), (2, 3))
UNPACK_FIRST = 12
RG_LATE = 0
THROTTLE = 1
WD_LATE = 1
SIB_AT = 0
W_LATE = 0
PARTS = ((0, 1280, ("x", "y", "z")), (1280, 1152, ("y", "z", "x")), (2432, 1152, ("z", "x", "y")))
WIDTHS = tuple(w for _, w, _ in PARTS)


def row_of(owner, s, t):
    own = jnp.broadcast_to(owner, s.shape)
    served = (iota(s.shape, 1) // 8) * 16 + (own // 16) * 2 + t + 1
    found = jnp.sum(jnp.where(own == s, served, 0), axis=1, keepdims=True)
    below = jnp.sum(jnp.where(own < s, 1, 0), axis=1, keepdims=True)
    return jnp.where(found > 0, found - 1, 128 + (s[:, :1] - below) * 2 + t[:, :1])


def kernel(
    owner, lengths, ids, owner_hbm, queries_hbm, fresh_hbm, res_hbm, gain_hbm, router_hbm, cache, w_value, w_out, w_gate, w_up, w_down, out,
    owner_row, queries, fresh, res, gain, router, cv, csend, crecv, qf, qs, q1, q2s, q3, sbuf, acc, att, c1, wvr, wr, hv, hvr, ys, yr,
    rtile, rg, ag, nat, hid, marks, chosen, wg, wu, wd, wrt, facc, mid, combine, base, turns,
    ya, yb, yc, r1a, r1b, r1c, t1a, t1b, t1c, r2a, r2b, r2c, t2a, t2b, t2c, r3a, r3b, r3c, z16,
    ld, cs, cr, q1ss, q1r, q2ss, q3r, a1s, a1r, vs, vr, vbs, vbr, ws, wrr, hs, hr, yss, yrr,
    rgs, rgr, rbs, rbr, ags, agr, abs_, abr, wds, wdr, ms, mr, rs, rr, zs, zr,
):
    n = lax.axis_index("node")
    l = lax.axis_index("local")
    core = n % 2
    at = {"z": n // 2, "y": l // 4, "x": l % 4}
    sib = (at["z"] * 2 + 1 - core, l)
    is_home = (at["x"] + at["y"]) % 2 == core
    mine = at["y"] * 2 + at["x"] // 2

    everything = pl.ds(0, 4)

    def peer(axis, p):
        if axis == "z":
            return (p * 2 + core, l)
        if axis == "y":
            return (n, p * 4 + at["x"])
        return (n, at["y"] * 4 + p)

    def slab(buf, order, q, s, val, c=None):
        idx = []
        for a in "zyx":
            if a in order[:s]:
                idx.append(everything)
            elif a == order[s]:
                idx.append(val)
            else:
                idx.append(at[a])
        return buf.at[core if c is None else c, q, idx[0], idx[1], idx[2]]

    def by_core(order, body):
        if isinstance(order[0], str):
            body(order)
        else:
            for c in range(2):
                pl.when(core == c)(functools.partial(body, order[c]))

    def gather_start(buf, orders, ss, rs_, q, s):
        def body(order):
            a = order[s]
            own = slab(buf, order, q, s, at[a])
            for j in range(1, 4):
                p = (at[a] + j) % 4
                send(own, own, ss.at[q, s, p], rs_.at[q, s, at[a]], peer(a, p))
        by_core(orders[q], body)

    def gather_wait(buf, orders, rs_, q, s):
        def body(order):
            a = order[s]
            for j in range(1, 4):
                p = (at[a] + j) % 4
                landed(slab(buf, order, q, s, p), rs_.at[q, s, p])
        by_core(orders[q], body)

    def gather_drain(buf, orders, ss):
        for q in range(4):
            def body(order, q=q):
                for s in range(3):
                    a = order[s]
                    for j in range(1, 4):
                        p = (at[a] + j) % 4
                        landed(slab(buf, order, q, s, at[a]), ss.at[q, s, p])
            by_core(orders[q], body)

    bar = pltpu.get_barrier_semaphore()

    def hello(device):
        pl.semaphore_signal(bar, 1, device_id=device, device_id_type=MESH)
    each(1, 16, lambda j: hello((n, (l + j) % 16)))
    each(1, 8, lambda j: hello(((n + j) % 8, l)))

    small = ((queries_hbm, queries), (fresh_hbm, fresh), (res_hbm, res), (owner_hbm, owner_row))
    for j, (src, dst) in enumerate(small):
        keep(src, dst, ld.at[4 + j])
    keep(cache, cv, ld.at[0])
    keep(router_hbm, router, ld.at[8])
    keep(gain_hbm, gain, ld.at[9])

    @pl.when(is_home & (mine != n))
    def _():
        each(0, 16, lambda j: hello((mine, j)))
    keep(w_value, wvr.at[at["z"], core], vr.at[at["z"]])
    keep(w_out.at[:, pl.ds(pl.multiple_of(n * 896, 128), 896)], wr.at[n], wrr.at[n])
    keep(w_gate, wg, ld.at[1])
    keep(w_up, wu, ld.at[2])
    own_cols = pl.ds(pl.multiple_of(core * 3584, 128), 3584)
    sib_cols = pl.ds(pl.multiple_of((1 - core) * 3584, 128), 3584)
    keep(w_down.at[:, own_cols], wd.at[0], ld.at[3])

    def deal_queries(pair):
        for k in range(8):
            lanes = pl.ds(pl.multiple_of((k * 8 + pair) * 1152, 128), 1152)
            v = queries[:, lanes].astype(F32)
            qf[pair * 2, k * 2:k * 2 + 2, :576] = v[:, :576]
            qf[pair * 2 + 1, k * 2:k * 2 + 2, :576] = v[:, 576:]
    for j, (src, dst) in enumerate(small):
        landed(dst, ld.at[4 + j])
    each(0, 8, deal_queries)
    qs[:, :, :576] = qf[:, :, :576].astype(BF)
    qs[:, :, 576:] = jnp.zeros((16, 16, 64), BF)
    own_band = iota((16, 576), 1) // 64 == iota((16, 576), 0)
    fold = (iota((576, 64), 0) % 64 == iota((576, 64), 1)).astype(BF)
    new = fresh[...].astype(F32)
    for t in range(2):
        bands = jnp.where(own_band, jnp.broadcast_to(new[t:t + 1], (16, 576)), 0.0).astype(BF)
        qs[t, :, 576:640] = jnp.dot(bands, fold, preferred_element_type=F32).astype(BF)

    pl.semaphore_wait(bar, 29)

    keep(qs.at[l], q1.at[l], q1r.at[l])

    def q_first(j):
        p = (l + j) % 16
        send(qs.at[p], q1.at[l], q1ss.at[p], q1r.at[l], (n, p))
    each(1, 16, q_first)
    landed(cv, ld.at[0])

    def cache_pick(t):
        pick = jnp.int32(0)
        for i in range(8):
            pick = jnp.where(owner[n * 8 + i] // 16 == t, i, pick)
        csend[t] = cv[pick]
    each(0, 8, cache_pick)

    def cache_send(i):
        dx = jnp.where(is_home, EVEN[i][0], ODD[i][0])
        dy = jnp.where(is_home, EVEN[i][1], ODD[i][1])
        px, py = (at["x"] + dx) % 4, (at["y"] + dy) % 4
        t, dest = py * 2 + px // 2, py * 4 + px

        @pl.when(dest == l)
        def _():
            keep(csend.at[t], crecv.at[l], cr.at[l])

        @pl.when(dest != l)
        def _():
            send(csend.at[t], crecv.at[l], cs.at[t], cr.at[l], (n, dest))
    for i in range(CACHE_FIRST):
        cache_send(i)

    def v_send():
        for j in range(1, 4):
            p = (at["z"] + j) % 4
            send(w_value, wvr.at[at["z"], core], vs.at[p], vr.at[at["z"]], peer("z", p))
    if V_EARLY:
        v_send()

    r = res[...].astype(F32)
    line = iota((16, 896), 0)
    tile = jnp.zeros((16, 896), F32)
    mark = jnp.zeros((16, 128), F32)
    for t in range(2):
        for k in range(8):
            tile = jnp.where(line == t * 8 + k, jnp.broadcast_to(r[t:t + 1, k * 896:(k + 1) * 896], (16, 896)), tile)
        hit = iota((16, 128), 1) == ids[t, 0]
        for j in range(1, 8):
            hit = hit | (iota((16, 128), 1) == ids[t, j])
        mark = jnp.where(hit & (iota((16, 128), 0) == t * 8), 1.0, mark)
    rtile[...] = jnp.concatenate([tile, mark], axis=1).astype(BF)
    for q in range(4):
        rg[core, q, at["z"], at["y"], at["x"]] = rtile[:, q * 256:(q + 1) * 256]
    if RG0_EARLY:
        for q in range(4):
            gather_start(rg, RESIDUAL, rgs, rgr, q, 0)

    each(0, 16, lambda j: landed(q1.at[j], q1r.at[j]))

    def q_second(j):
        p = (n + j) % 8
        pick = jnp.int32(0)
        for i in range(8):
            o = owner[p * 8 + i]
            pick = jnp.where(o // 16 == n, o % 16, pick)
        q2s[p] = q1[pick]
        dest = home_local(p, n)
        self_ = (p == n) & (dest == l)

        @pl.when(self_)
        def _():
            keep(q2s.at[p], q3.at[l], q3r.at[l])

        @pl.when(jnp.logical_not(self_))
        def _():
            send(q2s.at[p], q3.at[l], q2ss.at[p], q3r.at[l], (p, dest))
    each(0, 8, q_second)
    for i in range(CACHE_FIRST, 8):
        cache_send(i)

    if not V_EARLY:
        v_send()
    if not RG0_EARLY:
        for q in range(4):
            gather_start(rg, RESIDUAL, rgs, rgr, q, 0)

    def w_send(j):
        p = (n + j) % 8
        send(w_out.at[:, pl.ds(pl.multiple_of(p * 896, 128), 896)], wr.at[n], ws.at[p], wrr.at[n], (p, l))
    if not W_LATE:
        each(1, 8, w_send)

    def wd_send():
        send(w_down.at[:, sib_cols], wd.at[1], wds, wdr, sib)
    if not WD_LATE:
        wd_send()
    def rg1():
        for q in range(4):
            gather_wait(rg, RESIDUAL, rgr, q, 0)
            gather_start(rg, RESIDUAL, rgs, rgr, q, 1)

    def rg2(phase):
        for q in range(4):
            if RG2_AT[q] == phase:
                gather_wait(rg, RESIDUAL, rgr, q, 1)
                gather_start(rg, RESIDUAL, rgs, rgr, q, 2)
    if RG1_AT == 0:
        rg1()

    landed(router, ld.at[8])
    landed(gain, ld.at[9])
    wt = router[...]
    hi = wt.astype(BF)
    rest = wt - hi.astype(F32)
    mi = rest.astype(BF)
    wrt[0:16, :] = hi
    wrt[16:32, :] = mi
    wrt[32:48, :] = (rest - mi.astype(F32)).astype(BF)
    wrt[48:128, :] = jnp.zeros((80, 7168), BF)

    i64 = iota((256, 64), 0)
    spot = row_of(owner_row[...], i64 // 2, i64 % 2)
    to_nat = jnp.where(iota((256, 256), 1) == spot, 1.0, 0.0)
    turns[3] = to_nat.T.astype(BF)
    for k, (lo, width, order) in enumerate(PARTS):
        digit = {order[0]: i64 // 64, order[1]: i64 // 16 % 4, order[2]: i64 // 4 % 4}
        s64 = (digit["z"] * 2 + i64 // 2 % 2) * 16 + digit["y"] * 4 + digit["x"]
        turns[k] = (iota((256, 256), 1) == row_of(owner_row[...], s64, i64 % 2)).astype(BF)

    if W_LATE:
        each(1, 8, w_send)

    for j in range(4):
        landed(wvr.at[j, core], vr.at[j])
    send(wvr.at[:, core], wvr.at[:, core], vbs, vbr, sib)

    def cache_left(t):
        @pl.when(home_local(n, t) != l)
        def _():
            landed(csend.at[t], cs.at[t])
    if THROTTLE == 1:
        each(0, 8, cache_left)
    if RG1_AT == 1:
        rg1()
    rg2(0)

    @pl.when(is_home)
    def _():
        each(0, 16, lambda j: landed(q3.at[j], q3r.at[j]))
        length = jnp.int32(0)
        for i in range(8):
            r = n * 8 + i
            length = jnp.where(owner[r] // 16 == mine, lengths[r], length)
        q = q3[...].reshape(256, 640)[:, :576]
        spread = (iota((64, 576), 1) % 64 == iota((64, 576), 0)).astype(BF)
        rows = []
        for t in range(2):
            wide = jnp.dot(q3[t][:, 576:640], spread, preferred_element_type=F32)
            rows.append(jnp.sum(jnp.where(own_band, wide, 0.0), axis=0, keepdims=True))
        up = iota((128, 576), 0)
        fresh_rows = jnp.where(up == 0, rows[0], jnp.where(up == 1, rows[1], 0.0)).astype(BF)
        fs = lax.dot_general(q, fresh_rows, NT, preferred_element_type=F32) * score_scale
        fs = jnp.where(iota((256, 128), 1) <= iota((256, 128), 0) % 2, fs, -jnp.inf)

        def source(i, table):
            dx, dy = jnp.int32(table[0][0]), jnp.int32(table[0][1])
            for j in range(1, 8):
                dx = jnp.where(i == j, table[j][0], dx)
                dy = jnp.where(i == j, table[j][1], dy)
            return (at["y"] - dy + 4) % 4 * 4 + (at["x"] - dx + 4) % 4

        def score(p, top):
            le, lo = source(p, EVEN), source(p, ODD)
            landed(crecv.at[le], cr.at[le])
            landed(crecv.at[lo], cr.at[lo])
            keys = jnp.concatenate([crecv[le], crecv[lo]], axis=1)
            s = jnp.dot(q, keys, preferred_element_type=F32) * score_scale
            lane = iota((256, 256), 1)
            place = lane + jnp.where(lane < 128, le * 128, lo * 128 - 128)
            s = jnp.where(place < length, s, -jnp.inf)
            sbuf[p] = s
            return jnp.maximum(top, jnp.max(s, axis=1, keepdims=True))
        top = lax.fori_loop(0, 8, score, jnp.max(fs, axis=1, keepdims=True))
        fe = jnp.exp(fs - top)
        acc[...] = jnp.dot(fe.astype(BF), fresh_rows[:, :512], preferred_element_type=F32)

        def weigh(p, total):
            e = jnp.exp(sbuf[p] - top)
            le, lo = source(p, EVEN), source(p, ODD)
            values = jnp.concatenate([crecv[le, :512, :], crecv[lo, :512, :]], axis=1)
            acc[...] += lax.dot_general(e.astype(BF), values, NT, preferred_element_type=F32)
            return total + jnp.sum(e, axis=1, keepdims=True)
        total = lax.fori_loop(0, 8, weigh, jnp.sum(fe, axis=1, keepdims=True))
        att[...] = (acc[...] / total).astype(BF).reshape(16, 16, 512)

        keep(att.at[l], c1.at[mine], a1r.at[mine])

        def head_local(j):
            p = (l + j) % 16
            send(att.at[p], c1.at[mine], a1s.at[p], a1r.at[mine], (n, p))
        each(1, 16, head_local)

    if RG1_AT == 2:
        rg1()
    if WD_LATE:
        wd_send()
    rg2(1)

    landed(wvr.at[:, 1 - core], vbr)
    each(0, 8, lambda j: landed(c1.at[j], a1r.at[j]))
    rg2(5)
    to = iota((128, 128), 0)
    perm = (iota((128, 128), 1) == (to // 2 % 8) * 16 + (to // 16) * 2 + to % 2).astype(BF)
    by_head = jnp.dot(perm, c1[...].reshape(128, 512), preferred_element_type=F32).astype(BF)
    for k in range(8):
        hv[:, k * 128:(k + 1) * 128] = jnp.dot(
            by_head[k * 16:(k + 1) * 16], wvr[k // 2, k % 2], preferred_element_type=F32
        ).astype(BF)
    keep(hv, hvr.at[n], hr.at[n])

    def values_out(j):
        p = (n + j) % 8
        send(hv, hvr.at[n], hs.at[p], hr.at[n], (p, l))
    each(1, 8, values_out)
    rg2(2)

    def rg_sib(last):
        for q in range(4):
            if (RG2_AT[q] <= 1 and not SIB_AT) != last:
                gather_wait(rg, RESIDUAL, rgr, q, 2)
                send(rg.at[core, q], rg.at[core, q], rbs.at[q], rbr.at[q], sib)
    rg_sib(False)
    each(0, 8, lambda j: landed(wr.at[j], wrr.at[j]))
    each(0, 8, lambda j: landed(hvr.at[j], hr.at[j]))
    proj = jnp.dot(
        hvr[...].reshape(128, 1024), wr[...].reshape(1024, 896), preferred_element_type=F32
    ).reshape(16, 8, 896)
    high = jnp.concatenate([proj[:, :, 512:], jnp.zeros((16, 8, 128), F32)], axis=2)
    ys[...] = jnp.concatenate([proj[:, :, :512], high], axis=1).astype(BF)
    keep(ys.at[l], yr.at[l], yrr.at[l])

    def rows_out(j):
        p = (l + j) % 16
        send(ys.at[p], yr.at[l], yss.at[p], yrr.at[l], (n, p))
    each(1, 16, rows_out)
    rg2(3)

    deal = (iota((128, 128), 1) == (to % 16) * 8 + to // 16).astype(BF)

    def unpack(g):
        rows = pl.ds(pl.multiple_of(g * 16, 16), 16)
        z, c, y2 = g // 4, g // 2 % 2, g % 2
        x = jnp.concatenate(
            [rg[c, q, z, pl.ds(y2 * 2, 2)].reshape(128, 256) for q in range(4)], axis=1
        )
        d = jnp.dot(deal, x, preferred_element_type=F32).astype(BF)
        for k in range(8):
            nat[rows, k * 896:(k + 1) * 896] = d[k * 16:(k + 1) * 16, :896]
        marks[rows, :] = d[:16, 896:]

    def reorder(k):
        cols = pl.ds(pl.multiple_of(k * 896, 128), 896)
        hid[:, cols] = jnp.dot(turns[3], nat[:, cols], preferred_element_type=F32).astype(BF)

    def products(half, k, wide):
        cols = pl.ds(pl.multiple_of(k * 896, 128), 896)
        hg = (wide * gain[:, cols]).astype(BF)
        rows = pl.ds(half * 128, 128)
        facc[rows, :256] += jnp.dot(hg, wg[cols, :], preferred_element_type=F32)
        facc[rows, 256:512] += jnp.dot(hg, wu[cols, :], preferred_element_type=F32)
        facc[rows, 512:] += lax.dot_general(hg, wrt[:, cols], NT, preferred_element_type=F32)
        return jnp.sum(wide * wide, axis=1, keepdims=True)

    def activate(half, squares):
        rows = pl.ds(half * 128, 128)
        factor = lax.rsqrt(squares * (1.0 / 7168) + norm_eps)
        gated = facc[rows, :256] * factor
        lifted = facc[rows, 256:512] * factor
        mid[0, half] = (gated * jax.nn.sigmoid(gated) * lifted).astype(BF)
        send(mid.at[0, half], mid.at[1, half], ms.at[half], mr.at[half], sib)
        three = facc[rows, 512:]
        logits = three + pltpu.roll(three, 112, 1) + pltpu.roll(three, 96, 1)
        affinity = jax.nn.sigmoid(logits * factor)
        picked = jnp.where(chosen[rows, :] > 0.5, affinity, 0.0)
        share = picked / jnp.sum(picked, axis=1, keepdims=True) * route_scale
        combine[rows, :] = share.astype(BF)

    def resting(k, squares):
        cols = pl.ds(pl.multiple_of(k * 896, 128), 896)
        return squares + products(1, k, hid[128:, cols].astype(F32))

    facc[...] = jnp.zeros_like(facc)
    if UNPACK_FIRST:
        rg_sib(True)
        for q in range(4):
            landed(rg.at[1 - core, q], rbr.at[q])
    each(0, UNPACK_FIRST, unpack)
    each(0, 16, lambda j: landed(yr.at[j], yrr.at[j]))
    tot = yr[0].astype(F32)
    for j in range(1, 16):
        tot = tot + yr[j].astype(F32)
    shard = tot.astype(BF)
    for q in range(4):
        ag[core, q, at["z"], at["y"], at["x"]] = shard[:, q * 128:(q + 1) * 128]
        gather_start(ag, GATHER, ags, agr, q, 0)
    def forward(q, j, order):
        p = (at[order[2]] + j) % 4
        piece = slab(ag, order, q, 2, p)
        send(piece, piece, abs_.at[q, p], abr.at[q, p], sib)

    def forwarded(q, order):
        for p in range(4):
            landed(slab(ag, order, q, 2, p, 1 - core), abr.at[q, p])

    def forward_left(q, order):
        for p in range(4):
            landed(slab(ag, order, q, 2, p), abs_.at[q, p])

    def rg_landed():
        rg_sib(True)
        for q in range(4):
            landed(rg.at[1 - core, q], rbr.at[q])
    if RG_LATE == 0:
        if not UNPACK_FIRST:
            rg_landed()
        each(UNPACK_FIRST, 16, unpack)
    for q in range(4):
        gather_wait(ag, GATHER, agr, q, 0)
        gather_start(ag, GATHER, ags, agr, q, 1)
    if RG_LATE == 1:
        rg_landed()
        each(0, 16, unpack)
    if RG_LATE <= 1:
        each(0, 8, reorder)
    for q in range(4):
        gather_wait(ag, GATHER, agr, q, 1)
        gather_start(ag, GATHER, ags, agr, q, 2)
        by_core(GATHER[q], functools.partial(forward, q, 0))
    if RG_LATE == 2:
        rg_landed()
        each(0, 16, unpack)
        each(0, 8, reorder)
    chosen[...] = jnp.dot(turns[3], marks[...], preferred_element_type=F32)
    landed(wg, ld.at[1])
    landed(wu, ld.at[2])
    activate(1, lax.fori_loop(0, 8, resting, jnp.zeros((128, 1), F32)))
    def last_slabs(q, order):
        for j in range(1, 4):
            p = (at[order[2]] + j) % 4
            landed(slab(ag, order, q, 2, p), agr.at[q, 2, p])
            forward(q, j, order)
    for q in range(4):
        by_core(GATHER[q], functools.partial(last_slabs, q))

    def serving(c):
        def step(z, squares):
            tops, lows = [], []
            for q in range(4):
                b = ag[c, q, z].reshape(16, 16, 128).astype(F32)
                tops.append(b[:, :8].reshape(128, 128))
                lows.append(b[:, 8:].reshape(128, 128))
            attn = jnp.concatenate(tops + lows[:3], axis=1)
            k = z * 2 + c
            cols = pl.ds(pl.multiple_of(k * 896, 128), 896)
            h = (hid[:128, cols].astype(F32) + attn).astype(BF)
            hid[:128, cols] = h
            return squares + products(0, k, h.astype(F32))
        return step
    squares = lax.fori_loop(0, 4, serving(core), jnp.zeros((128, 1), F32))
    for q in range(4):
        order = GATHER[q]
        by_core(order if isinstance(order[0], str) else order[::-1], functools.partial(forwarded, q))
    activate(0, lax.fori_loop(0, 4, serving(1 - core), squares))

    lane = iota((256, 128), 1)
    e_own, e_sib = n * 2 + l // 8, sib[0] * 2 + l // 8
    landed(wd.at[0], ld.at[3])
    landed(wd.at[1], wdr)

    ybuf, r1, t1 = (ya, yb, yc), (r1a, r1b, r1c), (t1a, t1b, t1c)
    r2, t2, r3 = (r2a, r2b, r2c), (t2a, t2b, t2c), (r3a, r3b, r3c)
    turned = []
    for k in range(3):
        m0 = jnp.dot(turns[k], mid[0].reshape(256, 256), preferred_element_type=F32).astype(BF)
        turned.append((m0, jnp.dot(turns[k], combine[...], preferred_element_type=F32)))
    for half in range(2):
        landed(mid.at[1, half], mr.at[half])
    for k, (lo, width, order) in enumerate(PARTS):
        m0, cw = turned[k]
        m1 = jnp.dot(turns[k], mid[1].reshape(256, 256), preferred_element_type=F32).astype(BF)
        w0 = jnp.sum(jnp.where(lane == e_own, cw, 0.0), axis=1, keepdims=True)
        w1 = jnp.sum(jnp.where(lane == e_sib, cw, 0.0), axis=1, keepdims=True)
        cn = 384 if width % 384 == 0 else 640
        for c0 in range(0, width, cn):
            a = jnp.dot(m0, wd[0, :, lo + c0:lo + c0 + cn], preferred_element_type=F32) * w0
            b = jnp.dot(m1, wd[1, :, lo + c0:lo + c0 + cn], preferred_element_type=F32) * w1
            ybuf[k][:, :, c0:c0 + cn] = (a + b).astype(BF).reshape(4, 64, cn)
        a1 = order[0]
        for j in range(1, 4):
            p = (at[a1] + j) % 4
            send(ybuf[k].at[p], r1[k].at[at[a1]], rs.at[k, 0, p], rr.at[k, 0, at[a1]], peer(a1, p))

    s16 = iota((16, 64), 0) * 0 + (n * 16 + l)
    own_rows = row_of(owner_row[...], s16, iota((16, 64), 0) % 2)
    sel = (iota((16, 256), 1) == own_rows).astype(BF)
    for k in range(4):
        base[:, k * 1792:(k + 1) * 1792] = jnp.dot(
            sel, hid[:, k * 1792:(k + 1) * 1792], preferred_element_type=F32
        )

    for k, (lo, width, order) in enumerate(PARTS):
        a1, a2 = order[0], order[1]
        tot = ybuf[k][at[a1]].astype(F32)
        for j in range(1, 4):
            p = (at[a1] + j) % 4
            landed(r1[k].at[p], rr.at[k, 0, p])
            tot = tot + r1[k][p].astype(F32)
        t1[k][...] = tot.astype(BF).reshape(4, 16, width)
        for j in range(1, 4):
            p = (at[a2] + j) % 4
            send(t1[k].at[p], r2[k].at[at[a2]], rs.at[k, 1, p], rr.at[k, 1, at[a2]], peer(a2, p))
    for k, (lo, width, order) in enumerate(PARTS):
        a2, a3 = order[1], order[2]
        tot = t1[k][at[a2]].astype(F32)
        for j in range(1, 4):
            p = (at[a2] + j) % 4
            landed(r2[k].at[p], rr.at[k, 1, p])
            tot = tot + r2[k][p].astype(F32)
        t2[k][...] = tot.astype(BF)
        for j in range(1, 4):
            p = (at[a3] + j) % 4
            send(t2[k], r3[k].at[at[a3]], rs.at[k, 2, p], rr.at[k, 2, at[a3]], peer(a3, p))
    for k, (lo, width, order) in enumerate(PARTS):
        a3 = order[2]
        tot = t2[k][...].astype(F32)
        for j in range(1, 4):
            p = (at[a3] + j) % 4
            landed(r3[k].at[p], rr.at[k, 2, p])
            tot = tot + r3[k][p].astype(F32)
        z16[core, :, lo:lo + width] = tot.astype(BF)
    send(z16.at[core], z16.at[core], zs, zr, sib)
    landed(z16.at[1 - core], zr)

    up, dn = iota((16, 16), 0), iota((16, 16), 1)
    for half in range(2):
        for k, (lo, width, order) in enumerate(PARTS):
            c0 = half * 3584 + lo
            pickz = ((up < 2) & (dn == at[order[2]] * 4 + core * 2 + up)).astype(BF)
            mix = jnp.dot(pickz, z16[half, :, lo:lo + width], preferred_element_type=F32)
            out[:, c0:c0 + width] = (base[:, c0:c0 + width] + mix)[:2].astype(BF)

    def drain(j):
        p = (l + j) % 16
        landed(qs.at[p], q1ss.at[p])
        landed(ys.at[p], yss.at[p])

        @pl.when(is_home)
        def _():
            landed(att.at[p], a1s.at[p])
    each(1, 16, drain)

    def drain_home(t):
        if THROTTLE == 0:
            cache_left(t)

        @pl.when(jnp.logical_not((t == n) & (home_local(t, n) == l)))
        def _():
            landed(q2s.at[t], q2ss.at[t])
    each(0, 8, drain_home)

    def drain_node(j):
        p = (n + j) % 8
        landed(hv, hs.at[p])
        landed(wr.at[p], ws.at[p])
    each(1, 8, drain_node)
    for j in range(1, 4):
        p = (at["z"] + j) % 4
        landed(wvr.at[p, core], vs.at[p])
    landed(wvr.at[:, core], vbs)
    gather_drain(rg, RESIDUAL, rgs)
    gather_drain(ag, GATHER, ags)
    for q in range(4):
        landed(rg.at[core, q], rbs.at[q])
        by_core(GATHER[q], functools.partial(forward_left, q))
    landed(wd.at[1], wds)
    for half in range(2):
        landed(mid.at[0, half], ms.at[half])
    landed(z16.at[core], zs)
    for k, (lo, width, order) in enumerate(PARTS):
        for s, buf in enumerate((ybuf[k], t1[k], t2[k])):
            for j in range(1, 4):
                p = (at[order[s]] + j) % 4
                landed(buf if s == 2 else buf.at[p], rs.at[k, s, p])


def layer(owner, lengths, ids, queries, fresh, res, gain, router, cache, w_value, w_out, w_gate, w_up, w_down):
    dma = pltpu.SemaphoreType.DMA
    vm = pl.BlockSpec(memory_space=pltpu.VMEM)
    sm = pl.BlockSpec(memory_space=pltpu.SMEM)
    hbm = pl.BlockSpec(memory_space=pl.ANY)
    bf = lambda *shape: pltpu.VMEM(shape, BF)
    f32 = lambda *shape: pltpu.VMEM(shape, F32)
    return pl.pallas_call(
        kernel,
        name="layer",
        out_shape=jax.ShapeDtypeStruct((2, 7168), BF),
        in_specs=[sm, sm, sm] + [hbm] * 12,
        out_specs=vm,
        scratch_shapes=[
            pltpu.VMEM((1, 64), jnp.int32), bf(2, 73728), bf(2, 576), bf(2, 7168), f32(1, 7168), f32(16, 7168),
            bf(8, 576, 128), bf(8, 576, 128), bf(16, 576, 128),
            f32(16, 16, 640), bf(16, 16, 640), bf(16, 16, 640), bf(8, 16, 640), bf(16, 16, 640),
            f32(8, 256, 256), f32(256, 512), bf(16, 16, 512), bf(8, 16, 512),
            bf(4, 2, 512, 128), bf(8, 128, 896), bf(16, 1024), bf(8, 16, 1024),
            bf(16, 16, 512), bf(16, 16, 512),
            bf(16, 1024), bf(2, 4, 4, 4, 4, 16, 256), bf(2, 4, 4, 4, 4, 16, 128),
            bf(256, 7168), bf(256, 7168), bf(256, 128), f32(256, 128),
            bf(7168, 256), bf(7168, 256), bf(2, 256, 3584), bf(128, 7168),
            f32(256, 640), bf(2, 2, 128, 256), bf(256, 128), f32(16, 7168), bf(4, 256, 256),
        ]
        + [bf(4, 64, w) for w in WIDTHS] + [bf(4, 64, w) for w in WIDTHS]
        + [bf(4, 16, w) for w in WIDTHS] + [bf(4, 16, w) for w in WIDTHS]
        + [bf(16, w) for w in WIDTHS] + [bf(4, 16, w) for w in WIDTHS]
        + [bf(2, 16, 3584)]
        + [dma((k,)) for k in (10, 8, 16, 16, 16, 8, 16, 16, 8, 4, 4)]
        + [dma, dma]
        + [dma((k,)) for k in (8, 8, 8, 8, 16, 16)]
        + [
            dma((4, 3, 4)), dma((4, 3, 4)), dma((4,)), dma((4,)),
            dma((4, 3, 4)), dma((4, 3, 4)), dma((4, 4)), dma((4, 4)),
            dma, dma, dma((2,)), dma((2,)), dma((3, 3, 4)), dma((3, 3, 4)), dma, dma,
        ],
        compiler_params=pltpu.CompilerParams(
            collective_id=0, has_side_effects=True, vmem_limit_bytes=58 << 20
        ),
    )(owner, lengths, ids, owner[None, :], queries, fresh, res, gain, router, cache, w_value, w_out, w_gate, w_up, w_down)


def shards(
    latent_cache, lengths, owner_map, queries, new_latent, residual, w_value, w_out,
    norm_gain, w_router, expert_ids, w_gate, w_up, w_down,
):
    out = layer(
        owner_map, lengths, expert_ids[0], queries[0], new_latent[0], residual[0], norm_gain[None, :], w_router.T,
        latent_cache, w_value[0], w_out, w_gate, w_up, w_down,
    )
    return out[None]


def solution(mesh):
    both = ("node", "local")
    in_specs = (
        P("node", None, "local"), P(), P(), P(both, None, None), P(both, None, None),
        P(both, None, None), P(both, None, None), P(both, None), P(), P(),
        P(both, None, None), P(None, both), P(None, both), P(both, None),
    )
    return jax.shard_map(
        shards, mesh=mesh, in_specs=in_specs, out_specs=P(both, None, None), check_vma=False
    )
```

```python
import functools

import jax
import jax.numpy as jnp
from jax import lax
from jax.experimental import pallas as pl
from jax.experimental.pallas import tpu as pltpu
from jax.sharding import PartitionSpec as P

MESH = pl.DeviceIdType.MESH
BF = jnp.bfloat16
F32 = jnp.float32
score_scale = 192.0 ** (-0.5)
route_scale = 2.5
norm_eps = 1e-06
NT = (((1,), (1,)), ((), ()))


def iota(shape, dim):
    return lax.broadcasted_iota(jnp.int32, shape, dim)


def landed(ref, sem):
    pltpu.make_async_copy(ref, ref, sem).wait()


def send(src, dst, send_sem, recv_sem, device):
    pltpu.make_async_remote_copy(
        src_ref=src, dst_ref=dst, send_sem=send_sem, recv_sem=recv_sem,
        device_id=device, device_id_type=MESH,
    ).start()


def keep(src, dst, sem):
    pltpu.make_async_copy(src, dst, sem).start()


def home_local(node, target):
    row = target // 2
    return row * 4 + (target % 2) * 2 + (row + node) % 2


def each(lo, hi, body):
    def step(i, carry):
        body(i)
        return carry
    lax.fori_loop(lo, hi, step, 0)


GATHER = (("y", "z", "x"), ("z", "x", "y"), ("x", "y", "z"), (("y", "z", "x"), ("z", "x", "y")))
RESIDUAL = (("z", "y", "x"), ("z", "x", "y"), ("z", "y", "x"), ("z", "x", "y"))
CACHE_FIRST = 5
RG0_EARLY = 1
V_EARLY = 1
RG1_AT = 1
RG2_AT = (1, 1, 1, 1)
EVEN = ((1, 1), (3, 3), (1, 3), (3, 1), (2, 0), (0, 2), (2, 2), (0, 0))
ODD = ((1, 0), (3, 0), (0, 1), (0, 3), (1, 2), (3, 2), (2, 1), (2, 3))
UNPACK_FIRST = 12
RG_LATE = 0
THROTTLE = 1
WD_LATE = 1
SIB_AT = 0
W_LATE = 0
PARTS = ((0, 1280, ("x", "y", "z")), (1280, 1152, ("y", "z", "x")), (2432, 1152, ("z", "x", "y")))
WIDTHS = tuple(w for _, w, _ in PARTS)


def row_of(owner, s, t):
    own = jnp.broadcast_to(owner, s.shape)
    served = (iota(s.shape, 1) // 8) * 16 + (own // 16) * 2 + t + 1
    found = jnp.sum(jnp.where(own == s, served, 0), axis=1, keepdims=True)
    below = jnp.sum(jnp.where(own < s, 1, 0), axis=1, keepdims=True)
    return jnp.where(found > 0, found - 1, 128 + (s[:, :1] - below) * 2 + t[:, :1])


def kernel(
    owner, lengths, ids, owner_hbm, queries_hbm, fresh_hbm, res_hbm, gain_hbm, router_hbm, cache, w_value, w_out, w_gate, w_up, w_down, out,
    owner_row, queries, fresh, res, gain, router, cv, csend, crecv, qf, qs, q1, q2s, q3, sbuf, acc, att, c1, wvr, wr, hv, hvr, ys, yr,
    rtile, rg, ag, nat, hid, marks, chosen, wg, wu, wd, wrt, facc, mid, combine, base, turns,
    ya, yb, yc, r1a, r1b, r1c, t1a, t1b, t1c, r2a, r2b, r2c, t2a, t2b, t2c, r3a, r3b, r3c, z16,
    ld, cs, cr, q1ss, q1r, q2ss, q3r, a1s, a1r, vs, vr, vbs, vbr, ws, wrr, hs, hr, yss, yrr,
    rgs, rgr, rbs, rbr, ags, agr, abs_, abr, wds, wdr, ms, mr, rs, rr, zs, zr,
):
    n = lax.axis_index("node")
    l = lax.axis_index("local")
    core = n % 2
    at = {"z": n // 2, "y": l // 4, "x": l % 4}
    sib = (at["z"] * 2 + 1 - core, l)
    is_home = (at["x"] + at["y"]) % 2 == core
    mine = at["y"] * 2 + at["x"] // 2

    everything = pl.ds(0, 4)

    def peer(axis, p):
        if axis == "z":
            return (p * 2 + core, l)
        if axis == "y":
            return (n, p * 4 + at["x"])
        return (n, at["y"] * 4 + p)

    def slab(buf, order, q, s, val, c=None):
        idx = []
        for a in "zyx":
            if a in order[:s]:
                idx.append(everything)
            elif a == order[s]:
                idx.append(val)
            else:
                idx.append(at[a])
        return buf.at[core if c is None else c, q, idx[0], idx[1], idx[2]]

    def by_core(order, body):
        if isinstance(order[0], str):
            body(order)
        else:
            for c in range(2):
                pl.when(core == c)(functools.partial(body, order[c]))

    def gather_start(buf, orders, ss, rs_, q, s):
        def body(order):
            a = order[s]
            own = slab(buf, order, q, s, at[a])
            for j in range(1, 4):
                p = (at[a] + j) % 4
                send(own, own, ss.at[q, s, p], rs_.at[q, s, at[a]], peer(a, p))
        by_core(orders[q], body)

    def gather_wait(buf, orders, rs_, q, s):
        def body(order):
            a = order[s]
            for j in range(1, 4):
                p = (at[a] + j) % 4
                landed(slab(buf, order, q, s, p), rs_.at[q, s, p])
        by_core(orders[q], body)

    def gather_drain(buf, orders, ss):
        for q in range(4):
            def body(order, q=q):
                for s in range(3):
                    a = order[s]
                    for j in range(1, 4):
                        p = (at[a] + j) % 4
                        landed(slab(buf, order, q, s, at[a]), ss.at[q, s, p])
            by_core(orders[q], body)

    bar = pltpu.get_barrier_semaphore()

    def hello(device):
        pl.semaphore_signal(bar, 1, device_id=device, device_id_type=MESH)
    each(1, 16, lambda j: hello((n, (l + j) % 16)))
    each(1, 8, lambda j: hello(((n + j) % 8, l)))

    small = ((queries_hbm, queries), (fresh_hbm, fresh), (res_hbm, res), (owner_hbm, owner_row))
    for j, (src, dst) in enumerate(small):
        keep(src, dst, ld.at[4 + j])
    keep(cache, cv, ld.at[0])
    keep(router_hbm, router, ld.at[8])
    keep(gain_hbm, gain, ld.at[9])

    @pl.when(is_home & (mine != n))
    def _():
        each(0, 16, lambda j: hello((mine, j)))
    keep(w_value, wvr.at[at["z"], core], vr.at[at["z"]])
    keep(w_out.at[:, pl.ds(pl.multiple_of(n * 896, 128), 896)], wr.at[n], wrr.at[n])
    keep(w_gate, wg, ld.at[1])
    keep(w_up, wu, ld.at[2])
    own_cols = pl.ds(pl.multiple_of(core * 3584, 128), 3584)
    sib_cols = pl.ds(pl.multiple_of((1 - core) * 3584, 128), 3584)
    keep(w_down.at[:, own_cols], wd.at[0], ld.at[3])

    def deal_queries(pair):
        for k in range(8):
            lanes = pl.ds(pl.multiple_of((k * 8 + pair) * 1152, 128), 1152)
            v = queries[:, lanes].astype(F32)
            qf[pair * 2, k * 2:k * 2 + 2, :576] = v[:, :576]
            qf[pair * 2 + 1, k * 2:k * 2 + 2, :576] = v[:, 576:]
    for j, (src, dst) in enumerate(small):
        landed(dst, ld.at[4 + j])
    each(0, 8, deal_queries)
    qs[:, :, :576] = qf[:, :, :576].astype(BF)
    qs[:, :, 576:] = jnp.zeros((16, 16, 64), BF)
    own_band = iota((16, 576), 1) // 64 == iota((16, 576), 0)
    fold = (iota((576, 64), 0) % 64 == iota((576, 64), 1)).astype(BF)
    new = fresh[...].astype(F32)
    for t in range(2):
        bands = jnp.where(own_band, jnp.broadcast_to(new[t:t + 1], (16, 576)), 0.0).astype(BF)
        qs[t, :, 576:640] = jnp.dot(bands, fold, preferred_element_type=F32).astype(BF)

    pl.semaphore_wait(bar, 29)

    keep(qs.at[l], q1.at[l], q1r.at[l])

    def q_first(j):
        p = (l + j) % 16
        send(qs.at[p], q1.at[l], q1ss.at[p], q1r.at[l], (n, p))
    each(1, 16, q_first)
    landed(cv, ld.at[0])

    def cache_pick(t):
        pick = jnp.int32(0)
        for i in range(8):
            pick = jnp.where(owner[n * 8 + i] // 16 == t, i, pick)
        csend[t] = cv[pick]
    each(0, 8, cache_pick)

    def cache_send(i):
        dx = jnp.where(is_home, EVEN[i][0], ODD[i][0])
        dy = jnp.where(is_home, EVEN[i][1], ODD[i][1])
        px, py = (at["x"] + dx) % 4, (at["y"] + dy) % 4
        t, dest = py * 2 + px // 2, py * 4 + px

        @pl.when(dest == l)
        def _():
            keep(csend.at[t], crecv.at[l], cr.at[l])

        @pl.when(dest != l)
        def _():
            send(csend.at[t], crecv.at[l], cs.at[t], cr.at[l], (n, dest))
    for i in range(CACHE_FIRST):
        cache_send(i)

    def v_send():
        for j in range(1, 4):
            p = (at["z"] + j) % 4
            send(w_value, wvr.at[at["z"], core], vs.at[p], vr.at[at["z"]], peer("z", p))
    if V_EARLY:
        v_send()

    r = res[...].astype(F32)
    line = iota((16, 896), 0)
    tile = jnp.zeros((16, 896), F32)
    mark = jnp.zeros((16, 128), F32)
    for t in range(2):
        for k in range(8):
            tile = jnp.where(line == t * 8 + k, jnp.broadcast_to(r[t:t + 1, k * 896:(k + 1) * 896], (16, 896)), tile)
        hit = iota((16, 128), 1) == ids[t, 0]
        for j in range(1, 8):
            hit = hit | (iota((16, 128), 1) == ids[t, j])
        mark = jnp.where(hit & (iota((16, 128), 0) == t * 8), 1.0, mark)
    rtile[...] = jnp.concatenate([tile, mark], axis=1).astype(BF)
    for q in range(4):
        rg[core, q, at["z"], at["y"], at["x"]] = rtile[:, q * 256:(q + 1) * 256]
    if RG0_EARLY:
        for q in range(4):
            gather_start(rg, RESIDUAL, rgs, rgr, q, 0)

    each(0, 16, lambda j: landed(q1.at[j], q1r.at[j]))

    def q_second(j):
        p = (n + j) % 8
        pick = jnp.int32(0)
        for i in range(8):
            o = owner[p * 8 + i]
            pick = jnp.where(o // 16 == n, o % 16, pick)
        q2s[p] = q1[pick]
        dest = home_local(p, n)
        self_ = (p == n) & (dest == l)

        @pl.when(self_)
        def _():
            keep(q2s.at[p], q3.at[l], q3r.at[l])

        @pl.when(jnp.logical_not(self_))
        def _():
            send(q2s.at[p], q3.at[l], q2ss.at[p], q3r.at[l], (p, dest))
    each(0, 8, q_second)
    for i in range(CACHE_FIRST, 8):
        cache_send(i)

    if not V_EARLY:
        v_send()
    if not RG0_EARLY:
        for q in range(4):
            gather_start(rg, RESIDUAL, rgs, rgr, q, 0)

    def w_send(j):
        p = (n + j) % 8
        send(w_out.at[:, pl.ds(pl.multiple_of(p * 896, 128), 896)], wr.at[n], ws.at[p], wrr.at[n], (p, l))
    if not W_LATE:
        each(1, 8, w_send)

    def wd_send():
        send(w_down.at[:, sib_cols], wd.at[1], wds, wdr, sib)
    if not WD_LATE:
        wd_send()
    def rg1():
        for q in range(4):
            gather_wait(rg, RESIDUAL, rgr, q, 0)
            gather_start(rg, RESIDUAL, rgs, rgr, q, 1)

    def rg2(phase):
        for q in range(4):
            if RG2_AT[q] == phase:
                gather_wait(rg, RESIDUAL, rgr, q, 1)
                gather_start(rg, RESIDUAL, rgs, rgr, q, 2)
    if RG1_AT == 0:
        rg1()

    landed(router, ld.at[8])
    landed(gain, ld.at[9])
    wt = router[...]
    hi = wt.astype(BF)
    rest = wt - hi.astype(F32)
    mi = rest.astype(BF)
    wrt[0:16, :] = hi
    wrt[16:32, :] = mi
    wrt[32:48, :] = (rest - mi.astype(F32)).astype(BF)
    wrt[48:128, :] = jnp.zeros((80, 7168), BF)

    i64 = iota((256, 64), 0)
    spot = row_of(owner_row[...], i64 // 2, i64 % 2)
    to_nat = jnp.where(iota((256, 256), 1) == spot, 1.0, 0.0)
    turns[3] = to_nat.T.astype(BF)
    for k, (lo, width, order) in enumerate(PARTS):
        digit = {order[0]: i64 // 64, order[1]: i64 // 16 % 4, order[2]: i64 // 4 % 4}
        s64 = (digit["z"] * 2 + i64 // 2 % 2) * 16 + digit["y"] * 4 + digit["x"]
        turns[k] = (iota((256, 256), 1) == row_of(owner_row[...], s64, i64 % 2)).astype(BF)

    if W_LATE:
        each(1, 8, w_send)

    for j in range(4):
        landed(wvr.at[j, core], vr.at[j])
    send(wvr.at[:, core], wvr.at[:, core], vbs, vbr, sib)

    def cache_left(t):
        @pl.when(home_local(n, t) != l)
        def _():
            landed(csend.at[t], cs.at[t])
    if THROTTLE == 1:
        each(0, 8, cache_left)
    if RG1_AT == 1:
        rg1()
    rg2(0)

    @pl.when(is_home)
    def _():
        each(0, 16, lambda j: landed(q3.at[j], q3r.at[j]))
        length = jnp.int32(0)
        for i in range(8):
            r = n * 8 + i
            length = jnp.where(owner[r] // 16 == mine, lengths[r], length)
        q = q3[...].reshape(256, 640)[:, :576]
        spread = (iota((64, 576), 1) % 64 == iota((64, 576), 0)).astype(BF)
        rows = []
        for t in range(2):
            wide = jnp.dot(q3[t][:, 576:640], spread, preferred_element_type=F32)
            rows.append(jnp.sum(jnp.where(own_band, wide, 0.0), axis=0, keepdims=True))
        up = iota((128, 576), 0)
        fresh_rows = jnp.where(up == 0, rows[0], jnp.where(up == 1, rows[1], 0.0)).astype(BF)
        fs = lax.dot_general(q, fresh_rows, NT, preferred_element_type=F32) * score_scale
        fs = jnp.where(iota((256, 128), 1) <= iota((256, 128), 0) % 2, fs, -jnp.inf)

        def source(i, table):
            dx, dy = jnp.int32(table[0][0]), jnp.int32(table[0][1])
            for j in range(1, 8):
                dx = jnp.where(i == j, table[j][0], dx)
                dy = jnp.where(i == j, table[j][1], dy)
            return (at["y"] - dy + 4) % 4 * 4 + (at["x"] - dx + 4) % 4

        def score(p, top):
            le, lo = source(p, EVEN), source(p, ODD)
            landed(crecv.at[le], cr.at[le])
            landed(crecv.at[lo], cr.at[lo])
            keys = jnp.concatenate([crecv[le], crecv[lo]], axis=1)
            s = jnp.dot(q, keys, preferred_element_type=F32) * score_scale
            lane = iota((256, 256), 1)
            place = lane + jnp.where(lane < 128, le * 128, lo * 128 - 128)
            s = jnp.where(place < length, s, -jnp.inf)
            sbuf[p] = s
            return jnp.maximum(top, jnp.max(s, axis=1, keepdims=True))
        top = lax.fori_loop(0, 8, score, jnp.max(fs, axis=1, keepdims=True))
        fe = jnp.exp(fs - top)
        acc[...] = jnp.dot(fe.astype(BF), fresh_rows[:, :512], preferred_element_type=F32)

        def weigh(p, total):
            e = jnp.exp(sbuf[p] - top)
            le, lo = source(p, EVEN), source(p, ODD)
            values = jnp.concatenate([crecv[le, :512, :], crecv[lo, :512, :]], axis=1)
            acc[...] += lax.dot_general(e.astype(BF), values, NT, preferred_element_type=F32)
            return total + jnp.sum(e, axis=1, keepdims=True)
        total = lax.fori_loop(0, 8, weigh, jnp.sum(fe, axis=1, keepdims=True))
        att[...] = (acc[...] / total).astype(BF).reshape(16, 16, 512)

        keep(att.at[l], c1.at[mine], a1r.at[mine])

        def head_local(j):
            p = (l + j) % 16
            send(att.at[p], c1.at[mine], a1s.at[p], a1r.at[mine], (n, p))
        each(1, 16, head_local)

    if RG1_AT == 2:
        rg1()
    if WD_LATE:
        wd_send()
    rg2(1)

    landed(wvr.at[:, 1 - core], vbr)
    each(0, 8, lambda j: landed(c1.at[j], a1r.at[j]))
    rg2(5)
    to = iota((128, 128), 0)
    perm = (iota((128, 128), 1) == (to // 2 % 8) * 16 + (to // 16) * 2 + to % 2).astype(BF)
    by_head = jnp.dot(perm, c1[...].reshape(128, 512), preferred_element_type=F32).astype(BF)
    for k in range(8):
        hv[:, k * 128:(k + 1) * 128] = jnp.dot(
            by_head[k * 16:(k + 1) * 16], wvr[k // 2, k % 2], preferred_element_type=F32
        ).astype(BF)
    keep(hv, hvr.at[n], hr.at[n])

    def values_out(j):
        p = (n + j) % 8
        send(hv, hvr.at[n], hs.at[p], hr.at[n], (p, l))
    each(1, 8, values_out)
    rg2(2)

    def rg_sib(last):
        for q in range(4):
            if (RG2_AT[q] <= 1 and not SIB_AT) != last:
                gather_wait(rg, RESIDUAL, rgr, q, 2)
                send(rg.at[core, q], rg.at[core, q], rbs.at[q], rbr.at[q], sib)
    rg_sib(False)
    each(0, 8, lambda j: landed(wr.at[j], wrr.at[j]))
    each(0, 8, lambda j: landed(hvr.at[j], hr.at[j]))
    proj = jnp.dot(
        hvr[...].reshape(128, 1024), wr[...].reshape(1024, 896), preferred_element_type=F32
    ).reshape(16, 8, 896)
    high = jnp.concatenate([proj[:, :, 512:], jnp.zeros((16, 8, 128), F32)], axis=2)
    ys[...] = jnp.concatenate([proj[:, :, :512], high], axis=1).astype(BF)
    keep(ys.at[l], yr.at[l], yrr.at[l])

    def rows_out(j):
        p = (l + j) % 16
        send(ys.at[p], yr.at[l], yss.at[p], yrr.at[l], (n, p))
    each(1, 16, rows_out)
    rg2(3)

    deal = (iota((128, 128), 1) == (to % 16) * 8 + to // 16).astype(BF)

    def unpack(g):
        rows = pl.ds(pl.multiple_of(g * 16, 16), 16)
        z, c, y2 = g // 4, g // 2 % 2, g % 2
        x = jnp.concatenate(
            [rg[c, q, z, pl.ds(y2 * 2, 2)].reshape(128, 256) for q in range(4)], axis=1
        )
        d = jnp.dot(deal, x, preferred_element_type=F32).astype(BF)
        for k in range(8):
            nat[rows, k * 896:(k + 1) * 896] = d[k * 16:(k + 1) * 16, :896]
        marks[rows, :] = d[:16, 896:]

    def reorder(k):
        cols = pl.ds(pl.multiple_of(k * 896, 128), 896)
        hid[:, cols] = jnp.dot(turns[3], nat[:, cols], preferred_element_type=F32).astype(BF)

    def products(half, k, wide):
        cols = pl.ds(pl.multiple_of(k * 896, 128), 896)
        hg = (wide * gain[:, cols]).astype(BF)
        rows = pl.ds(half * 128, 128)
        facc[rows, :256] += jnp.dot(hg, wg[cols, :], preferred_element_type=F32)
        facc[rows, 256:512] += jnp.dot(hg, wu[cols, :], preferred_element_type=F32)
        facc[rows, 512:] += lax.dot_general(hg, wrt[:, cols], NT, preferred_element_type=F32)
        return jnp.sum(wide * wide, axis=1, keepdims=True)

    def activate(half, squares):
        rows = pl.ds(half * 128, 128)
        factor = lax.rsqrt(squares * (1.0 / 7168) + norm_eps)
        gated = facc[rows, :256] * factor
        lifted = facc[rows, 256:512] * factor
        mid[0, half] = (gated * jax.nn.sigmoid(gated) * lifted).astype(BF)
        send(mid.at[0, half], mid.at[1, half], ms.at[half], mr.at[half], sib)
        three = facc[rows, 512:]
        logits = three + pltpu.roll(three, 112, 1) + pltpu.roll(three, 96, 1)
        affinity = jax.nn.sigmoid(logits * factor)
        picked = jnp.where(chosen[rows, :] > 0.5, affinity, 0.0)
        share = picked / jnp.sum(picked, axis=1, keepdims=True) * route_scale
        combine[rows, :] = share.astype(BF)

    def resting(k, squares):
        cols = pl.ds(pl.multiple_of(k * 896, 128), 896)
        return squares + products(1, k, hid[128:, cols].astype(F32))

    facc[...] = jnp.zeros_like(facc)
    if UNPACK_FIRST:
        rg_sib(True)
        for q in range(4):
            landed(rg.at[1 - core, q], rbr.at[q])
    each(0, UNPACK_FIRST, unpack)
    each(0, 16, lambda j: landed(yr.at[j], yrr.at[j]))
    tot = yr[0].astype(F32)
    for j in range(1, 16):
        tot = tot + yr[j].astype(F32)
    shard = tot.astype(BF)
    for q in range(4):
        ag[core, q, at["z"], at["y"], at["x"]] = shard[:, q * 128:(q + 1) * 128]
        gather_start(ag, GATHER, ags, agr, q, 0)
    def forward(q, j, order):
        p = (at[order[2]] + j) % 4
        piece = slab(ag, order, q, 2, p)
        send(piece, piece, abs_.at[q, p], abr.at[q, p], sib)

    def forwarded(q, order):
        for p in range(4):
            landed(slab(ag, order, q, 2, p, 1 - core), abr.at[q, p])

    def forward_left(q, order):
        for p in range(4):
            landed(slab(ag, order, q, 2, p), abs_.at[q, p])

    def rg_landed():
        rg_sib(True)
        for q in range(4):
            landed(rg.at[1 - core, q], rbr.at[q])
    if RG_LATE == 0:
        if not UNPACK_FIRST:
            rg_landed()
        each(UNPACK_FIRST, 16, unpack)
    for q in range(4):
        gather_wait(ag, GATHER, agr, q, 0)
        gather_start(ag, GATHER, ags, agr, q, 1)
    if RG_LATE == 1:
        rg_landed()
        each(0, 16, unpack)
    if RG_LATE <= 1:
        each(0, 8, reorder)
    for q in range(4):
        gather_wait(ag, GATHER, agr, q, 1)
        gather_start(ag, GATHER, ags, agr, q, 2)
        by_core(GATHER[q], functools.partial(forward, q, 0))
    if RG_LATE == 2:
        rg_landed()
        each(0, 16, unpack)
        each(0, 8, reorder)
    chosen[...] = jnp.dot(turns[3], marks[...], preferred_element_type=F32)
    landed(wg, ld.at[1])
    landed(wu, ld.at[2])
    activate(1, lax.fori_loop(0, 8, resting, jnp.zeros((128, 1), F32)))
    def last_slabs(q, order):
        for j in range(1, 4):
            p = (at[order[2]] + j) % 4
            landed(slab(ag, order, q, 2, p), agr.at[q, 2, p])
            forward(q, j, order)
    for q in range(4):
        by_core(GATHER[q], functools.partial(last_slabs, q))

    def serving(c):
        def step(z, squares):
            tops, lows = [], []
            for q in range(4):
                b = ag[c, q, z].reshape(16, 16, 128).astype(F32)
                tops.append(b[:, :8].reshape(128, 128))
                lows.append(b[:, 8:].reshape(128, 128))
            attn = jnp.concatenate(tops + lows[:3], axis=1)
            k = z * 2 + c
            cols = pl.ds(pl.multiple_of(k * 896, 128), 896)
            h = (hid[:128, cols].astype(F32) + attn).astype(BF)
            hid[:128, cols] = h
            return squares + products(0, k, h.astype(F32))
        return step
    squares = lax.fori_loop(0, 4, serving(core), jnp.zeros((128, 1), F32))
    for q in range(4):
        order = GATHER[q]
        by_core(order if isinstance(order[0], str) else order[::-1], functools.partial(forwarded, q))
    activate(0, lax.fori_loop(0, 4, serving(1 - core), squares))

    lane = iota((256, 128), 1)
    e_own, e_sib = n * 2 + l // 8, sib[0] * 2 + l // 8
    landed(wd.at[0], ld.at[3])
    landed(wd.at[1], wdr)

    ybuf, r1, t1 = (ya, yb, yc), (r1a, r1b, r1c), (t1a, t1b, t1c)
    r2, t2, r3 = (r2a, r2b, r2c), (t2a, t2b, t2c), (r3a, r3b, r3c)
    turned = []
    for k in range(3):
        m0 = jnp.dot(turns[k], mid[0].reshape(256, 256), preferred_element_type=F32).astype(BF)
        turned.append((m0, jnp.dot(turns[k], combine[...], preferred_element_type=F32)))
    for half in range(2):
        landed(mid.at[1, half], mr.at[half])
    for k, (lo, width, order) in enumerate(PARTS):
        m0, cw = turned[k]
        m1 = jnp.dot(turns[k], mid[1].reshape(256, 256), preferred_element_type=F32).astype(BF)
        w0 = jnp.sum(jnp.where(lane == e_own, cw, 0.0), axis=1, keepdims=True)
        w1 = jnp.sum(jnp.where(lane == e_sib, cw, 0.0), axis=1, keepdims=True)
        cn = 384 if width % 384 == 0 else 640
        for c0 in range(0, width, cn):
            a = jnp.dot(m0, wd[0, :, lo + c0:lo + c0 + cn], preferred_element_type=F32) * w0
            b = jnp.dot(m1, wd[1, :, lo + c0:lo + c0 + cn], preferred_element_type=F32) * w1
            ybuf[k][:, :, c0:c0 + cn] = (a + b).astype(BF).reshape(4, 64, cn)
        a1 = order[0]
        for j in range(1, 4):
            p = (at[a1] + j) % 4
            send(ybuf[k].at[p], r1[k].at[at[a1]], rs.at[k, 0, p], rr.at[k, 0, at[a1]], peer(a1, p))

    s16 = iota((16, 64), 0) * 0 + (n * 16 + l)
    own_rows = row_of(owner_row[...], s16, iota((16, 64), 0) % 2)
    sel = (iota((16, 256), 1) == own_rows).astype(BF)
    for k in range(4):
        base[:, k * 1792:(k + 1) * 1792] = jnp.dot(
            sel, hid[:, k * 1792:(k + 1) * 1792], preferred_element_type=F32
        )

    for k, (lo, width, order) in enumerate(PARTS):
        a1, a2 = order[0], order[1]
        tot = ybuf[k][at[a1]].astype(F32)
        for j in range(1, 4):
            p = (at[a1] + j) % 4
            landed(r1[k].at[p], rr.at[k, 0, p])
            tot = tot + r1[k][p].astype(F32)
        t1[k][...] = tot.astype(BF).reshape(4, 16, width)
        for j in range(1, 4):
            p = (at[a2] + j) % 4
            send(t1[k].at[p], r2[k].at[at[a2]], rs.at[k, 1, p], rr.at[k, 1, at[a2]], peer(a2, p))
    for k, (lo, width, order) in enumerate(PARTS):
        a2, a3 = order[1], order[2]
        tot = t1[k][at[a2]].astype(F32)
        for j in range(1, 4):
            p = (at[a2] + j) % 4
            landed(r2[k].at[p], rr.at[k, 1, p])
            tot = tot + r2[k][p].astype(F32)
        t2[k][...] = tot.astype(BF)
        for j in range(1, 4):
            p = (at[a3] + j) % 4
            send(t2[k], r3[k].at[at[a3]], rs.at[k, 2, p], rr.at[k, 2, at[a3]], peer(a3, p))
    for k, (lo, width, order) in enumerate(PARTS):
        a3 = order[2]
        tot = t2[k][...].astype(F32)
        for j in range(1, 4):
            p = (at[a3] + j) % 4
            landed(r3[k].at[p], rr.at[k, 2, p])
            tot = tot + r3[k][p].astype(F32)
        z16[core, :, lo:lo + width] = tot.astype(BF)
        piece = z16.at[core, :, pl.ds(lo, width)]
        send(piece, piece, zs.at[k], zr.at[k], sib)

    up, dn = iota((16, 16), 0), iota((16, 16), 1)
    for k, (lo, width, order) in enumerate(PARTS):
        landed(z16.at[1 - core, :, pl.ds(lo, width)], zr.at[k])
        for half in range(2):
            c0 = half * 3584 + lo
            pickz = ((up < 2) & (dn == at[order[2]] * 4 + core * 2 + up)).astype(BF)
            mix = jnp.dot(pickz, z16[half, :, lo:lo + width], preferred_element_type=F32)
            out[:, c0:c0 + width] = (base[:, c0:c0 + width] + mix)[:2].astype(BF)

    def drain(j):
        p = (l + j) % 16
        landed(qs.at[p], q1ss.at[p])
        landed(ys.at[p], yss.at[p])

        @pl.when(is_home)
        def _():
            landed(att.at[p], a1s.at[p])
    each(1, 16, drain)

    def drain_home(t):
        if THROTTLE == 0:
            cache_left(t)

        @pl.when(jnp.logical_not((t == n) & (home_local(t, n) == l)))
        def _():
            landed(q2s.at[t], q2ss.at[t])
    each(0, 8, drain_home)

    def drain_node(j):
        p = (n + j) % 8
        landed(hv, hs.at[p])
        landed(wr.at[p], ws.at[p])
    each(1, 8, drain_node)
    for j in range(1, 4):
        p = (at["z"] + j) % 4
        landed(wvr.at[p, core], vs.at[p])
    landed(wvr.at[:, core], vbs)
    gather_drain(rg, RESIDUAL, rgs)
    gather_drain(ag, GATHER, ags)
    for q in range(4):
        landed(rg.at[core, q], rbs.at[q])
        by_core(GATHER[q], functools.partial(forward_left, q))
    landed(wd.at[1], wds)
    for half in range(2):
        landed(mid.at[0, half], ms.at[half])
    for k, (lo, width, order) in enumerate(PARTS):
        landed(z16.at[core, :, pl.ds(lo, width)], zs.at[k])
    for k, (lo, width, order) in enumerate(PARTS):
        for s, buf in enumerate((ybuf[k], t1[k], t2[k])):
            for j in range(1, 4):
                p = (at[order[s]] + j) % 4
                landed(buf if s == 2 else buf.at[p], rs.at[k, s, p])


def layer(owner, lengths, ids, queries, fresh, res, gain, router, cache, w_value, w_out, w_gate, w_up, w_down):
    dma = pltpu.SemaphoreType.DMA
    vm = pl.BlockSpec(memory_space=pltpu.VMEM)
    sm = pl.BlockSpec(memory_space=pltpu.SMEM)
    hbm = pl.BlockSpec(memory_space=pl.ANY)
    bf = lambda *shape: pltpu.VMEM(shape, BF)
    f32 = lambda *shape: pltpu.VMEM(shape, F32)
    return pl.pallas_call(
        kernel,
        name="layer",
        out_shape=jax.ShapeDtypeStruct((2, 7168), BF),
        in_specs=[sm, sm, sm] + [hbm] * 12,
        out_specs=vm,
        scratch_shapes=[
            pltpu.VMEM((1, 64), jnp.int32), bf(2, 73728), bf(2, 576), bf(2, 7168), f32(1, 7168), f32(16, 7168),
            bf(8, 576, 128), bf(8, 576, 128), bf(16, 576, 128),
            f32(16, 16, 640), bf(16, 16, 640), bf(16, 16, 640), bf(8, 16, 640), bf(16, 16, 640),
            f32(8, 256, 256), f32(256, 512), bf(16, 16, 512), bf(8, 16, 512),
            bf(4, 2, 512, 128), bf(8, 128, 896), bf(16, 1024), bf(8, 16, 1024),
            bf(16, 16, 512), bf(16, 16, 512),
            bf(16, 1024), bf(2, 4, 4, 4, 4, 16, 256), bf(2, 4, 4, 4, 4, 16, 128),
            bf(256, 7168), bf(256, 7168), bf(256, 128), f32(256, 128),
            bf(7168, 256), bf(7168, 256), bf(2, 256, 3584), bf(128, 7168),
            f32(256, 640), bf(2, 2, 128, 256), bf(256, 128), f32(16, 7168), bf(4, 256, 256),
        ]
        + [bf(4, 64, w) for w in WIDTHS] + [bf(4, 64, w) for w in WIDTHS]
        + [bf(4, 16, w) for w in WIDTHS] + [bf(4, 16, w) for w in WIDTHS]
        + [bf(16, w) for w in WIDTHS] + [bf(4, 16, w) for w in WIDTHS]
        + [bf(2, 16, 3584)]
        + [dma((k,)) for k in (10, 8, 16, 16, 16, 8, 16, 16, 8, 4, 4)]
        + [dma, dma]
        + [dma((k,)) for k in (8, 8, 8, 8, 16, 16)]
        + [
            dma((4, 3, 4)), dma((4, 3, 4)), dma((4,)), dma((4,)),
            dma((4, 3, 4)), dma((4, 3, 4)), dma((4, 4)), dma((4, 4)),
            dma, dma, dma((2,)), dma((2,)), dma((3, 3, 4)), dma((3, 3, 4)), dma((3,)), dma((3,)),
        ],
        compiler_params=pltpu.CompilerParams(
            collective_id=0, has_side_effects=True, vmem_limit_bytes=58 << 20
        ),
    )(owner, lengths, ids, owner[None, :], queries, fresh, res, gain, router, cache, w_value, w_out, w_gate, w_up, w_down)


def shards(
    latent_cache, lengths, owner_map, queries, new_latent, residual, w_value, w_out,
    norm_gain, w_router, expert_ids, w_gate, w_up, w_down,
):
    out = layer(
        owner_map, lengths, expert_ids[0], queries[0], new_latent[0], residual[0], norm_gain[None, :], w_router.T,
        latent_cache, w_value[0], w_out, w_gate, w_up, w_down,
    )
    return out[None]


def solution(mesh):
    both = ("node", "local")
    in_specs = (
        P("node", None, "local"), P(), P(), P(both, None, None), P(both, None, None),
        P(both, None, None), P(both, None, None), P(both, None), P(), P(),
        P(both, None, None), P(None, both), P(None, both), P(both, None),
    )
    return jax.shard_map(
        shards, mesh=mesh, in_specs=in_specs, out_specs=P(both, None, None), check_vma=False
    )
```
